32 devices in a mesh: gx: 4 (over y, core), gy: 8 (over z, x).
Axes of the slice: x: 2, y: 2, z: 4, core: 2. Of those that a mesh axis runs over, the one named last changes fastest.
Arguments:
- inputs: bfloat16 [64, 128, 8, 256], P('gx', 'gy'), may hold values from -6 to 6
- preact: bfloat16 [64, 128, 8, 256], P('gx', 'gy'), may hold values from -6 to 6
- out_grad: bfloat16 [64, 128, 8, 256], P('gx', 'gy'), may hold values from -6 to 6
- weight_one: bfloat16 [6912, 256], P('gx', 'gy'), may hold values from -0.078125 to 0.078125
- weight_two: bfloat16 [6912, 256], P('gx', 'gy'), may hold values from -0.078125 to 0.078125
- occupancy: int32 [8, 16, 1], P('gx', 'gy'), may hold values from 0 to 1, as said below
Outputs:
- input_grad: bfloat16 [64, 128, 8, 256], P('gx', 'gy')
- weight_one_grad: float32 [6912, 256], P('gx', 'gy')
- weight_two_grad: float32 [6912, 256], P('gx', 'gy')
The draws below stay inside these ranges and needn't reach their ends.
Inputs may be any that keep to these rules, and one draw needn't show every extreme that they name: `occupancy`: among the 2 x 2 x 1 block of one device's tile at most 2 are occupied, and in every draw some device's tile has exactly 2.
All inputs are finite; a program needn't handle non-finite values.
Results may differ from the reference program's by a relative error of at most 0.005.
Values may be sent and summed in bfloat16 or wider, within the bound.
No kernel may reach another device: no remote copies, remote signals or barrier semaphores. Data moves between devices by JAX's collectives and lax.ppermute only.
A program may use at most 128 MiB of HBM per device.

```python
import jax
import jax.numpy as jnp
from jax import lax

C = 256
B = 8
BZ = 1
AMAX = 2
NX = 64
NY = 128
NZ = 8
KROWS = 6912
N_GX = 4
N_GY = 8


def draw_occupancy(key, part):
    devices_all = N_GX * N_GY
    per_device = 4 * BZ
    key_count, key_busy, key_order = jax.random.split(key, 3)
    counts = jax.random.randint(key_count, (devices_all,), 0, AMAX + 1)
    busiest = jax.random.randint(key_busy, (), 0, devices_all)
    counts = jnp.where(jnp.arange(devices_all) == busiest, AMAX, counts)
    order_rank = jax.vmap(lambda sub_key: jax.random.permutation(sub_key, per_device))(jax.random.split(key_order, devices_all))
    occupied = (order_rank < counts[:, None]).astype(jnp.int32)
    occupied = occupied.reshape(N_GX, N_GY, 2, 2, BZ).transpose(0, 2, 1, 3, 4)
    return occupied.reshape(2 * N_GX, 2 * N_GY, BZ)


def steps_of(own_key, dims, cuts, low, largest):
    def one(position, blocks):
        steps = jax.random.uniform(jax.random.fold_in(jax.random.fold_in(own_key, 6), position), (blocks,), jnp.float32, low / len(cuts), largest / len(cuts))
        return jnp.repeat(jnp.exp(steps), dims[position] // blocks).reshape((-1,) + (1,) * (len(dims) - position - 1))

    loudness = one(*cuts[0])
    for cut in cuts[1:]:
        loudness = loudness * one(*cut)
    return loudness


def centred(stream_key, extent, scale, reach, cuts=(), held_as=jnp.bfloat16):
    drawn = jax.random.normal(stream_key, extent, jnp.float32) * scale
    if len(cuts) > 0:
        drawn = steps_of(stream_key, extent, cuts, -0.22, 0.18) * drawn
    return jnp.clip(drawn, min=-reach, max=reach).astype(held_as)


def setup_inputs(seed: int = 0) -> dict:
    arg_keys = jax.random.split(jax.random.key(seed), 7)
    return {
        "inputs": centred(arg_keys[0], (NX, NY, NZ, C), 1.0, 6.0, ((0, 4), (1, 8))),
        "preact": centred(arg_keys[1], (NX, NY, NZ, C), 1.0, 6.0, ((0, 4), (1, 8))),
        "out_grad": centred(arg_keys[2], (NX, NY, NZ, C), 1.0, 6.0, ((0, 4), (1, 8))),
        "weight_one": centred(arg_keys[3], (KROWS, C), (27 * C) ** -0.5, 0.078125, ((0, 4), (1, 8))),
        "weight_two": centred(arg_keys[4], (KROWS, C), (27 * C) ** -0.5, 0.078125, ((0, 4), (1, 8))),
        "occupancy": draw_occupancy(jax.random.fold_in(arg_keys[6], 71), 0),
    }


stencil_taps = [(shift_x, shift_y, shift_z) for shift_x in (-1, 0, 1) for shift_y in (-1, 0, 1) for shift_z in (-1, 0, 1)]


def block_work(pad_in, pad_grad, weight, corner, valid, edge, totals):
    chans = pad_in.shape[-1]
    sizes = (edge + 2, edge + 2, edge + 2, chans)
    patch_in = lax.dynamic_slice(pad_in, corner, sizes)
    patch_grad = lax.dynamic_slice(pad_grad, corner, sizes)
    center = patch_grad[1:edge + 1, 1:edge + 1, 1:edge + 1, :].reshape(edge * edge * edge, chans)
    center = jnp.where(valid, center, jnp.zeros_like(center))
    back = jnp.zeros((edge * edge * edge, chans), jnp.float32)
    fresh = []
    for index, (shift_x, shift_y, shift_z) in enumerate(stencil_taps):
        piece_in = patch_in[1 + shift_x:1 + shift_x + edge, 1 + shift_y:1 + shift_y + edge, 1 + shift_z:1 + shift_z + edge, :].reshape(edge * edge * edge, chans)
        fresh.append(totals[index] + lax.dot_general(piece_in, center, (((0,), (0,)), ((), ())), preferred_element_type=jnp.float32))
        piece_grad = patch_grad[1 - shift_x:1 - shift_x + edge, 1 - shift_y:1 - shift_y + edge, 1 - shift_z:1 - shift_z + edge, :].reshape(edge * edge * edge, chans)
        tap_rows = weight[index * chans:(index + 1) * chans, :]
        back = back + lax.dot_general(piece_grad, tap_rows, (((1,), (1,)), ((), ())), preferred_element_type=jnp.float32)
    return tuple(fresh), back


def place(tile, values, corner, valid, edge):
    block = values.reshape(edge, edge, edge, values.shape[-1])
    old = lax.dynamic_slice(tile, corner, block.shape)
    return lax.dynamic_update_slice(tile, jnp.where(valid, block, old), corner)


def pad_space(field):
    return jnp.pad(field, ((1, 1), (1, 1), (1, 1), (0, 0)))


def reference(inputs, preact, out_grad, weight_one, weight_two, occupancy):
    edge = B
    chans = inputs.shape[-1]
    mask = jnp.repeat(jnp.repeat(jnp.repeat(occupancy, edge, 0), edge, 1), edge, 2)
    active = (mask > 0)[..., None]
    zero = jnp.zeros((), jnp.bfloat16)
    second_in = jnp.where(active & (preact > 0), preact, zero)
    first_in = jnp.where(active, inputs, zero)
    grad_two = jnp.where(active, out_grad, zero)
    pad_second = pad_space(second_in)
    pad_first = pad_space(first_in)
    pad_grad = pad_space(grad_two)
    flat = occupancy.reshape(-1)
    slots = N_GX * N_GY * AMAX
    found = jnp.nonzero(flat, size=slots, fill_value=0)[0].astype(jnp.int32)
    valid = jnp.arange(slots) < jnp.sum(flat)
    span_y = occupancy.shape[1]
    span_z = occupancy.shape[2]
    corner_x = (found // (span_y * span_z)) * edge
    corner_y = ((found // span_z) % span_y) * edge
    corner_z = (found % span_z) * edge
    anchor = jnp.zeros((), jnp.int32)
    empty_sums = tuple(jnp.zeros((chans, chans), jnp.float32) for _ in range(27))

    def first_pass(carry, item):
        totals, grad_tile = carry
        cx, cy, cz, okay = item
        corner = (cx, cy, cz, anchor)
        totals, back = block_work(pad_second, pad_grad, weight_two, corner, okay, edge, totals)
        pre_block = lax.dynamic_slice(preact, corner, (edge, edge, edge, chans)).reshape(edge * edge * edge, chans)
        gated = jnp.where(pre_block > 0, back, jnp.zeros_like(back)).astype(jnp.bfloat16)
        return (totals, place(grad_tile, gated, corner, okay, edge)), None

    start = (empty_sums, jnp.zeros(inputs.shape, jnp.bfloat16))
    (sums_two, grad_one), _ = lax.scan(first_pass, start, (corner_x, corner_y, corner_z, valid))
    pad_one = pad_space(grad_one)

    def second_pass(carry, item):
        totals, out_tile = carry
        cx, cy, cz, okay = item
        corner = (cx, cy, cz, anchor)
        totals, back = block_work(pad_first, pad_one, weight_one, corner, okay, edge, totals)
        return (totals, place(out_tile, back.astype(jnp.bfloat16), corner, okay, edge)), None

    start = (empty_sums, jnp.zeros(inputs.shape, jnp.bfloat16))
    (sums_one, input_grad), _ = lax.scan(second_pass, start, (corner_x, corner_y, corner_z, valid))
    scale = float(N_GX * N_GY * B ** 3) ** -0.5
    sum_one = jnp.concatenate(sums_one, axis=0)
    sum_two = jnp.concatenate(sums_two, axis=0)
    return input_grad, sum_one * scale, sum_two * scale
```

```python
import functools

import jax
import jax.numpy as jnp
from jax import lax
from jax.experimental import pallas as pl
from jax.experimental.pallas import tpu as pltpu
from jax.sharding import PartitionSpec as P

B = 8
AMAX = 2
LANES = 128
BOTH = ("gx", "gy")

stencil_columns = [(shift_x, shift_y) for shift_x in (-1, 0, 1) for shift_y in (-1, 0, 1)]


class Plan:
    def __init__(self, n_gx, n_gy, rows, chans):
        self.n_gx = n_gx
        self.n_gy = n_gy
        self.rows = rows
        self.chans = chans
        self.cols = chans // n_gy
        self.pair = 2 if n_gx % 2 == 0 else 1
        self.inner = 2 if n_gy % 2 == 0 else 1
        self.n_y = n_gx // self.pair
        self.n_z = n_gy // self.inner
        self.n_plane = self.n_y * self.inner
        self.tiles = 27 * chans // LANES
        self.first = [rows * i // LANES for i in range(n_gx)]
        self.offset = [rows * i % LANES for i in range(n_gx)]
        self.depth = max(-(-(self.offset[i] + rows) // LANES) for i in range(n_gx))

    def owners(self, tile):
        return [
            (i, tile - self.first[i])
            for i in range(self.n_gx)
            if tile * LANES < (i + 1) * self.rows and (tile + 1) * LANES > i * self.rows
        ]


def swap(x, plan, flip_gx, flip_gy):
    n_gy = plan.n_gy
    pairs = [
        (i * n_gy + j, (i ^ flip_gx) * n_gy + (j ^ flip_gy))
        for i in range(plan.n_gx)
        for j in range(n_gy)
    ]
    return lax.ppermute(x, BOTH, pairs)


def swap_plane(x, plan, slot):
    return swap(x, plan, slot // plan.inner * plan.pair, slot % plan.inner)


def swap_z(x, plan, slot):
    return swap(x, plan, 0, slot * plan.inner)


def pick_blocks(occ_ref, n_bx, n_by):
    count = jnp.int32(0)
    first = jnp.int32(0)
    second = jnp.int32(0)
    for i in range(n_bx * n_by):
        on = occ_ref[i] > 0
        first = jnp.where(jnp.logical_and(on, count == 0), i, first)
        second = jnp.where(jnp.logical_and(on, count == 1), i, second)
        count = count + on.astype(jnp.int32)
    blocks = []
    for slot, index in enumerate((first, second)):
        blocks.append((index // n_by, index % n_by, (count > slot).astype(jnp.int32)))
    return blocks


def block_mask(occ_ref, block, step_x, step_y, n_bx, n_by):
    bx = block[0] + step_x
    by = block[1] + step_y
    inside = (bx >= 0) & (bx < n_bx) & (by >= 0) & (by < n_by)
    at = jnp.clip(bx, 0, n_bx - 1) * n_by + jnp.clip(by, 0, n_by - 1)
    return jnp.where(inside, occ_ref[at], 1) * block[2]


def load_extended(tile_ref, low_x, high_x, low_y, high_y, ext_ref, sems):
    size_x, size_y = tile_ref.shape[:2]
    copies = [
        pltpu.make_async_copy(
            tile_ref, ext_ref.at[pl.ds(1, size_x), pl.ds(1, size_y)], sems.at[0]
        ),
        pltpu.make_async_copy(low_x, ext_ref.at[0, pl.ds(1, size_y)], sems.at[1]),
        pltpu.make_async_copy(high_x, ext_ref.at[size_x + 1, pl.ds(1, size_y)], sems.at[2]),
        pltpu.make_async_copy(low_y, ext_ref.at[:, 0], sems.at[3]),
        pltpu.make_async_copy(high_y, ext_ref.at[:, size_y + 1], sems.at[4]),
    ]
    for copy in copies:
        copy.start()
    for copy in copies:
        copy.wait()


def spread_patches(occ_ref, blocks, ext_ref, shifted_ref, n_bx, n_by, rectify):
    edge = B
    row = lax.broadcasted_iota(jnp.int32, (edge, ext_ref.shape[-1]), 0)

    def at_x(x, carry):
        step_x = jnp.where(x == 0, -1, jnp.where(x == edge + 1, 1, 0))
        masks = [
            [block_mask(occ_ref, block, step_x, step_y, n_bx, n_by) > 0 for step_y in (-1, 0, 1)]
            for block in blocks
        ]
        for y in range(edge + 2):
            side = 0 if y == 0 else (2 if y == edge + 1 else 1)
            planes = [[], [], []]
            for index, block in enumerate(blocks):
                value = ext_ref[block[0] * edge + x, block[1] * edge + y].astype(jnp.float32)
                if rectify:
                    value = jnp.maximum(value, 0.0)
                value = jnp.where(masks[index][side], value, 0.0)
                below = jnp.where(row == 0, 0.0, pltpu.roll(value, 1, 0))
                above = jnp.where(row == edge - 1, 0.0, pltpu.roll(value, edge - 1, 0))
                for plane, part in zip(planes, (below, value, above)):
                    plane.append(part)
            for j in range(3):
                shifted_ref[j, x, y] = jnp.concatenate(planes[j], axis=0).astype(jnp.bfloat16)
        return carry

    lax.fori_loop(0, edge + 2, at_x, 0)


def gather_blocks(blocks, tile_ref, center_ref):
    edge = B

    def at_x(x, carry):
        for y in range(edge):
            parts = []
            for block in blocks:
                value = tile_ref[block[0] * edge + x, block[1] * edge + y].astype(jnp.float32)
                parts.append(jnp.where(block[2] > 0, value, 0.0))
            center_ref[x, y] = jnp.concatenate(parts, axis=0).astype(jnp.bfloat16)
        return carry

    lax.fori_loop(0, edge, at_x, 0)


def window(shifted_ref, plane, start_x, start_y):
    edge = B
    piece = shifted_ref[plane, start_x : start_x + edge, start_y : start_y + edge]
    return piece.reshape(edge * edge * AMAX * edge, piece.shape[-1])


def weight_kernel(
    plan, n_bx, n_by, rectify, compact,
    occ_ref, pos_ref, tile_ref, low_x, high_x, low_y, high_y, grad_ref,
    out_ref,
    ext_ref, shifted_ref, center_ref, turned_ref, sems,
):
    blocks = pick_blocks(occ_ref, n_bx, n_by)
    load_extended(tile_ref, low_x, high_x, low_y, high_y, ext_ref, sems)
    spread_patches(occ_ref, blocks, ext_ref, shifted_ref, n_bx, n_by, rectify)
    if compact:
        center = grad_ref[...]
    else:
        gather_blocks(blocks, grad_ref, center_ref)
        center = center_ref[...]
    voxels = B * B * AMAX * B
    turned_ref[...] = center.reshape(voxels, plan.chans).astype(jnp.float32).T.astype(jnp.bfloat16)
    my_gx = pos_ref[0]
    my_gy = pos_ref[1]
    my_core = my_gx % plan.pair
    my_y = my_gx // plan.pair
    my_x = my_gy % plan.inner
    my_z = my_gy // plan.inner
    per_column = 3 * plan.chans // LANES
    for column, (shift_x, shift_y) in enumerate(stencil_columns):
        pieces = [window(shifted_ref, j, 1 + shift_x, 1 + shift_y) for j in range(3)]
        product = jnp.dot(
            turned_ref[...],
            jnp.concatenate(pieces, axis=1),
            preferred_element_type=jnp.float32,
        ).astype(jnp.bfloat16)
        for part in range(per_column):
            lanes = product[:, part * LANES : (part + 1) * LANES]
            for shard, place in plan.owners(column * per_column + part):
                core = (shard % plan.pair) ^ my_core
                y = (shard // plan.pair) ^ my_y
                for j in range(plan.n_gy):
                    slot = y * plan.inner + ((j % plan.inner) ^ my_x)
                    z = (j // plan.inner) ^ my_z
                    out_ref[core, slot, z, place] = lanes[j * plan.cols : (j + 1) * plan.cols]


def weight_sums(plan, occ, pos, tile, rim, grad, n_bx, n_by, rectify, compact):
    size_x, size_y, edge, chans = tile.shape
    smem = pl.BlockSpec(memory_space=pltpu.SMEM)
    anywhere = pl.BlockSpec(memory_space=pl.ANY)
    vmem = pl.BlockSpec(memory_space=pltpu.VMEM)
    voxels = B * B * AMAX * B
    shape = (plan.pair, plan.n_plane, plan.n_z, plan.depth, plan.cols, LANES)
    return pl.pallas_call(
        functools.partial(weight_kernel, plan, n_bx, n_by, rectify, compact),
        out_shape=jax.ShapeDtypeStruct(shape, jnp.bfloat16),
        in_specs=[smem, smem] + [anywhere] * 5 + [vmem],
        out_specs=vmem,
        scratch_shapes=[
            pltpu.VMEM((size_x + 2, size_y + 2, edge, chans), jnp.bfloat16),
            pltpu.VMEM((3, B + 2, B + 2, AMAX * B, chans), jnp.bfloat16),
            pltpu.VMEM((B, B, AMAX * B, chans), jnp.bfloat16),
            pltpu.VMEM((chans, voxels), jnp.bfloat16),
            pltpu.SemaphoreType.DMA((5,)),
        ],
        compiler_params=pltpu.CompilerParams(vmem_limit_bytes=40 * 1024 * 1024),
        cost_estimate=pl.CostEstimate(
            flops=2 * 27 * voxels * chans * chans, bytes_accessed=8 << 20, transcendentals=0
        ),
    )(occ, pos, tile, *rim, grad)


def data_kernel(
    plan, n_bx, n_by, gated, n_pieces,
    occ_ref, pos_ref, tile_ref, low_x, high_x, low_y, high_y, *rest,
):
    piece_refs = rest[:n_pieces]
    rest = rest[n_pieces:]
    if gated:
        gate_ref, out_ref, center_ref = rest[:3]
        rest = rest[3:]
    else:
        out_ref = rest[0]
        rest = rest[1:]
    ext_ref, shifted_ref, weight_ref, total_ref, sems, weight_sems = rest
    edge = B
    blocks = pick_blocks(occ_ref, n_bx, n_by)
    my_gx = pos_ref[0]
    my_gy = pos_ref[1]
    copies = []
    for piece in range(n_pieces):
        core = piece // plan.n_plane
        slot = piece % plan.n_plane
        shard = my_gx ^ (slot // plan.inner * plan.pair + core)
        for z in range(plan.n_z):
            column = my_gy ^ (z * plan.inner + slot % plan.inner)
            start = pl.multiple_of(column * plan.cols, plan.cols)
            copies.append(
                pltpu.make_async_copy(
                    piece_refs[piece].at[z],
                    weight_ref.at[shard, pl.ds(start, plan.cols)],
                    weight_sems.at[piece, z],
                )
            )
    for copy in copies:
        copy.start()
    load_extended(tile_ref, low_x, high_x, low_y, high_y, ext_ref, sems)
    spread_patches(occ_ref, blocks, ext_ref, shifted_ref, n_bx, n_by, False)
    out_ref[...] = jnp.zeros_like(out_ref)
    for copy in copies:
        copy.wait()

    def kernel_lanes(tile):
        total = None
        for shard, place in plan.owners(tile):
            part = weight_ref[shard, :, place * LANES : (place + 1) * LANES]
            total = part if total is None else total + part
        return total

    halves = plan.chans // LANES
    for column, (shift_x, shift_y) in enumerate(stencil_columns):
        pieces = [window(shifted_ref, 2 - j, 1 - shift_x, 1 - shift_y) for j in range(3)]
        taps = [
            jnp.concatenate(
                [kernel_lanes((3 * column + j) * halves + part) for part in range(halves)], axis=1
            )
            for j in range(3)
        ]
        product = jnp.dot(
            jnp.concatenate(pieces, axis=1),
            jnp.concatenate(taps, axis=0),
            preferred_element_type=jnp.float32,
        )
        if column == 0:
            total_ref[...] = product
        else:
            total_ref[...] += product

    def at_x(x, carry):
        for y in range(edge):
            kept = []
            for index, block in enumerate(blocks):
                start = pl.multiple_of((x * edge + y) * AMAX * edge, AMAX * edge) + index * edge
                value = total_ref[pl.ds(start, edge), :]
                at = (block[0] * edge + x, block[1] * edge + y)
                if gated:
                    value = jnp.where(gate_ref[at].astype(jnp.float32) > 0, value, 0.0)
                    value = jnp.where(block[2] > 0, value, 0.0)
                    kept.append(value)

                @pl.when(block[2] > 0)
                def _():
                    out_ref[at] = value.astype(jnp.bfloat16)

            if gated:
                center_ref[x, y] = jnp.concatenate(kept, axis=0).astype(jnp.bfloat16)
        return carry

    lax.fori_loop(0, edge, at_x, 0)


def data_grad(plan, occ, pos, tile, rim, pieces, n_bx, n_by, gate=None):
    size_x, size_y, edge, chans = tile.shape
    smem = pl.BlockSpec(memory_space=pltpu.SMEM)
    anywhere = pl.BlockSpec(memory_space=pl.ANY)
    vmem = pl.BlockSpec(memory_space=pltpu.VMEM)
    voxels = B * B * AMAX * B
    gated = gate is not None
    out_shape = [jax.ShapeDtypeStruct(tile.shape, jnp.bfloat16)]
    if gated:
        out_shape.append(jax.ShapeDtypeStruct((B, B, AMAX * B, chans), jnp.bfloat16))
    return pl.pallas_call(
        functools.partial(data_kernel, plan, n_bx, n_by, gated, len(pieces)),
        out_shape=out_shape,
        in_specs=[smem, smem] + [anywhere] * (5 + len(pieces)) + [vmem] * gated,
        out_specs=[vmem] * len(out_shape),
        scratch_shapes=[
            pltpu.VMEM((size_x + 2, size_y + 2, edge, chans), jnp.bfloat16),
            pltpu.VMEM((3, B + 2, B + 2, AMAX * B, chans), jnp.bfloat16),
            pltpu.VMEM((plan.n_gx, chans, plan.depth * LANES), jnp.bfloat16),
            pltpu.VMEM((voxels, chans), jnp.float32),
            pltpu.SemaphoreType.DMA((5,)),
            pltpu.SemaphoreType.DMA((len(pieces), plan.n_z)),
        ],
        compiler_params=pltpu.CompilerParams(vmem_limit_bytes=40 * 1024 * 1024),
        cost_estimate=pl.CostEstimate(
            flops=2 * 27 * voxels * chans * chans, bytes_accessed=8 << 20, transcendentals=0
        ),
    )(occ, pos, tile, *rim, *pieces, *([gate] if gated else []))


def offsets_of(plan):
    return jnp.asarray(plan.offset, jnp.int32)[lax.axis_index("gx")]


def gather_kernel(plan, weight):
    frame = jnp.zeros((plan.cols, plan.depth * LANES), weight.dtype)
    own = lax.dynamic_update_slice(frame, weight.T, (0, offsets_of(plan)))
    line = jnp.stack([own] + [swap_z(own, plan, slot) for slot in range(1, plan.n_z)])
    plane = [line] + [swap_plane(line, plan, slot) for slot in range(1, plan.n_plane)]
    other = [swap(part, plan, 1, 0) for part in plane] if plan.pair == 2 else []
    return plane + other


def reduce_kernel(plan, sums):
    total = [sums[0, slot].astype(jnp.float32) for slot in range(plan.n_plane)]
    if plan.pair == 2:
        got = swap(sums[1], plan, 1, 0)
        total = [total[slot] + got[slot].astype(jnp.float32) for slot in range(plan.n_plane)]
    got = [
        swap_plane(total[slot].astype(jnp.bfloat16), plan, slot)
        for slot in range(1, plan.n_plane)
    ]
    line = total[0]
    for part in got:
        line = line + part.astype(jnp.float32)
    got = [
        swap_z(line[slot].astype(jnp.bfloat16), plan, slot) for slot in range(1, plan.n_z)
    ]
    own = line[0]
    for part in got:
        own = own + part.astype(jnp.float32)
    scale = float(plan.n_gx * plan.n_gy * B**3) ** (-0.5)
    flat = (own * scale).transpose(0, 2, 1).reshape(plan.depth * LANES, plan.cols)
    return lax.dynamic_slice(flat, (offsets_of(plan), 0), (plan.rows, plan.cols))


def ring(axis):
    size = lax.axis_size(axis)
    up = [(i, i + 1) for i in range(size - 1)]
    return up, [(j, i) for i, j in up]


def rims(first_x, last_x, first_y, last_y):
    up, down = ring("gx")
    low_x = lax.ppermute(last_x, "gx", up)
    high_x = lax.ppermute(first_x, "gx", down)
    up, down = ring("gy")
    low_y = lax.ppermute(
        jnp.concatenate([low_x[:, -1:], last_y, high_x[:, -1:]], axis=1), "gy", up
    )
    high_y = lax.ppermute(
        jnp.concatenate([low_x[:, :1], first_y, high_x[:, :1]], axis=1), "gy", down
    )
    return low_x, high_x, low_y, high_y


def body(inputs, preact, out_grad, weight_one, weight_two, occupancy):
    n_bx, n_by = occupancy.shape[:2]
    plan = Plan(
        lax.axis_size("gx"), lax.axis_size("gy"), weight_one.shape[0], inputs.shape[-1]
    )
    occ = occupancy.reshape(-1)
    pos = jnp.stack([lax.axis_index("gx"), lax.axis_index("gy")]).astype(jnp.int32)
    on = occupancy[:, :, 0] > 0
    along_x = jnp.repeat(on, B, axis=0)[..., None, None]
    along_y = jnp.repeat(on, B, axis=1)[..., None, None]
    zero = jnp.zeros((), jnp.bfloat16)
    fields = (jnp.maximum(preact, zero), inputs, out_grad)
    edges = rims(
        jnp.stack([jnp.where(along_y[0], x[0], zero) for x in fields]),
        jnp.stack([jnp.where(along_y[-1], x[-1], zero) for x in fields]),
        jnp.stack([jnp.where(along_x[:, 0], x[:, 0], zero) for x in fields]),
        jnp.stack([jnp.where(along_x[:, -1], x[:, -1], zero) for x in fields]),
    )
    rim_second, rim_first, rim_grad = [tuple(edge[i] for edge in edges) for i in range(3)]
    pieces_two = gather_kernel(plan, weight_two)
    pieces_one = gather_kernel(plan, weight_one)
    sums_two = weight_sums(plan, occ, pos, preact, rim_second, out_grad, n_bx, n_by, True, False)
    grad_one, center = data_grad(
        plan, occ, pos, out_grad, rim_grad, pieces_two, n_bx, n_by, preact
    )
    sums_one = weight_sums(plan, occ, pos, inputs, rim_first, center, n_bx, n_by, False, True)
    edges = rims(
        grad_one[None, 0], grad_one[None, -1], grad_one[None, :, 0], grad_one[None, :, -1]
    )
    rim_one = tuple(edge[0] for edge in edges)
    (input_grad,) = data_grad(plan, occ, pos, grad_one, rim_one, pieces_one, n_bx, n_by)
    return (input_grad, reduce_kernel(plan, sums_one), reduce_kernel(plan, sums_two))


def solution(mesh):
    return jax.shard_map(
        body,
        mesh=mesh,
        in_specs=(
            P("gx", "gy", None, None),
            P("gx", "gy", None, None),
            P("gx", "gy", None, None),
            P("gx", "gy"),
            P("gx", "gy"),
            P("gx", "gy", None),
        ),
        out_specs=(P("gx", "gy", None, None), P("gx", "gy"), P("gx", "gy")),
        check_vma=False,
    )
```

```python
import functools

import jax
import jax.numpy as jnp
from jax import lax
from jax.experimental import pallas as pl
from jax.experimental.pallas import tpu as pltpu
from jax.sharding import PartitionSpec as P

B = 8
AMAX = 2
LANES = 128
BOTH = ("gx", "gy")
SMALL = pl.CostEstimate(flops=1, bytes_accessed=1, transcendentals=0)

stencil_columns = [(shift_x, shift_y) for shift_x in (-1, 0, 1) for shift_y in (-1, 0, 1)]


class Plan:
    def __init__(self, n_gx, n_gy, rows, chans):
        self.n_gx = n_gx
        self.n_gy = n_gy
        self.rows = rows
        self.chans = chans
        self.cols = chans // n_gy
        self.pair = 2 if n_gx % 2 == 0 else 1
        self.inner = 2 if n_gy % 2 == 0 else 1
        self.n_y = n_gx // self.pair
        self.n_z = n_gy // self.inner
        self.n_plane = self.n_y * self.inner
        self.tiles = 27 * chans // LANES
        self.first = [rows * i // LANES for i in range(n_gx)]
        self.offset = [rows * i % LANES for i in range(n_gx)]
        self.depth = max(-(-(self.offset[i] + rows) // LANES) for i in range(n_gx))

    def owners(self, tile):
        return [
            (i, tile - self.first[i])
            for i in range(self.n_gx)
            if tile * LANES < (i + 1) * self.rows and (tile + 1) * LANES > i * self.rows
        ]


def swap(x, plan, flip_gx, flip_gy):
    n_gy = plan.n_gy
    pairs = [
        (i * n_gy + j, (i ^ flip_gx) * n_gy + (j ^ flip_gy))
        for i in range(plan.n_gx)
        for j in range(n_gy)
    ]
    return lax.ppermute(x, BOTH, pairs)


def swap_plane(x, plan, slot):
    return swap(x, plan, slot // plan.inner * plan.pair, slot % plan.inner)


def swap_z(x, plan, slot):
    return swap(x, plan, 0, slot * plan.inner)


def pick_blocks(occ_ref, n_bx, n_by):
    count = jnp.int32(0)
    first = jnp.int32(0)
    second = jnp.int32(0)
    for i in range(n_bx * n_by):
        on = occ_ref[i // n_by, i % n_by, 0] > 0
        first = jnp.where(jnp.logical_and(on, count == 0), i, first)
        second = jnp.where(jnp.logical_and(on, count == 1), i, second)
        count = count + on.astype(jnp.int32)
    blocks = []
    for slot, index in enumerate((first, second)):
        blocks.append((index // n_by, index % n_by, (count > slot).astype(jnp.int32)))
    return blocks


def block_mask(occ_ref, block, step_x, step_y, n_bx, n_by):
    bx = block[0] + step_x
    by = block[1] + step_y
    inside = (bx >= 0) & (bx < n_bx) & (by >= 0) & (by < n_by)
    near = occ_ref[jnp.clip(bx, 0, n_bx - 1), jnp.clip(by, 0, n_by - 1), 0]
    return jnp.where(inside, near, 1) * block[2]


def load_extended(index, tile_ref, low_x, high_x, low_y, high_y, ext_ref, sems):
    size_x, size_y = tile_ref.shape[:2]
    copies = [
        pltpu.make_async_copy(
            tile_ref, ext_ref.at[pl.ds(1, size_x), pl.ds(1, size_y)], sems.at[0]
        ),
        pltpu.make_async_copy(low_x.at[index], ext_ref.at[0, pl.ds(1, size_y)], sems.at[1]),
        pltpu.make_async_copy(
            high_x.at[index], ext_ref.at[size_x + 1, pl.ds(1, size_y)], sems.at[2]
        ),
        pltpu.make_async_copy(low_y.at[index], ext_ref.at[:, 0], sems.at[3]),
        pltpu.make_async_copy(high_y.at[index], ext_ref.at[:, size_y + 1], sems.at[4]),
    ]
    for copy in copies:
        copy.start()
    for copy in copies:
        copy.wait()


def spread_patches(occ_ref, blocks, ext_ref, shifted_ref, n_bx, n_by, rectify):
    edge = B
    row = lax.broadcasted_iota(jnp.int32, (edge, ext_ref.shape[-1]), 0)

    def at_x(x, carry):
        step_x = jnp.where(x == 0, -1, jnp.where(x == edge + 1, 1, 0))
        masks = [
            [block_mask(occ_ref, block, step_x, step_y, n_bx, n_by) > 0 for step_y in (-1, 0, 1)]
            for block in blocks
        ]
        for y in range(edge + 2):
            side = 0 if y == 0 else (2 if y == edge + 1 else 1)
            planes = [[], [], []]
            for index, block in enumerate(blocks):
                value = ext_ref[block[0] * edge + x, block[1] * edge + y].astype(jnp.float32)
                if rectify:
                    value = jnp.maximum(value, 0.0)
                value = jnp.where(masks[index][side], value, 0.0)
                below = jnp.where(row == 0, 0.0, pltpu.roll(value, 1, 0))
                above = jnp.where(row == edge - 1, 0.0, pltpu.roll(value, edge - 1, 0))
                for plane, part in zip(planes, (below, value, above)):
                    plane.append(part)
            for j in range(3):
                shifted_ref[j, x, y] = jnp.concatenate(planes[j], axis=0).astype(jnp.bfloat16)
        return carry

    lax.fori_loop(0, edge + 2, at_x, 0)


def gather_blocks(blocks, tile_ref, center_ref):
    edge = B

    def at_x(x, carry):
        for y in range(edge):
            parts = []
            for block in blocks:
                value = tile_ref[block[0] * edge + x, block[1] * edge + y].astype(jnp.float32)
                parts.append(jnp.where(block[2] > 0, value, 0.0))
            center_ref[x, y] = jnp.concatenate(parts, axis=0).astype(jnp.bfloat16)
        return carry

    lax.fori_loop(0, edge, at_x, 0)


def window(shifted_ref, plane, start_x, start_y):
    edge = B
    piece = shifted_ref[plane, start_x : start_x + edge, start_y : start_y + edge]
    return piece.reshape(edge * edge * AMAX * edge, piece.shape[-1])


def weight_kernel(
    plan, n_bx, n_by, index, rectify, compact,
    occ_ref, tile_ref, low_x, high_x, low_y, high_y, grad_ref,
    *rest,
):
    *out_refs, ext_ref, shifted_ref, center_ref, turned_ref, sems = rest
    blocks = pick_blocks(occ_ref, n_bx, n_by)
    load_extended(index, tile_ref, low_x, high_x, low_y, high_y, ext_ref, sems)
    spread_patches(occ_ref, blocks, ext_ref, shifted_ref, n_bx, n_by, rectify)
    if compact:
        center = grad_ref[...]
    else:
        gather_blocks(blocks, grad_ref, center_ref)
        center = center_ref[...]
    voxels = B * B * AMAX * B
    turned_ref[...] = center.reshape(voxels, plan.chans).astype(jnp.float32).T.astype(jnp.bfloat16)
    my_gx = lax.axis_index("gx")
    my_gy = lax.axis_index("gy")
    my_core = my_gx % plan.pair
    my_y = my_gx // plan.pair
    my_x = my_gy % plan.inner
    my_z = my_gy // plan.inner
    per_column = 3 * plan.chans // LANES

    def products(core_here):
        for column, (shift_x, shift_y) in enumerate(stencil_columns):
            pieces = [window(shifted_ref, j, 1 + shift_x, 1 + shift_y) for j in range(3)]
            product = jnp.dot(
                turned_ref[...],
                jnp.concatenate(pieces, axis=1),
                preferred_element_type=jnp.float32,
            ).astype(jnp.bfloat16)
            for part in range(per_column):
                lanes = product[:, part * LANES : (part + 1) * LANES]
                for shard, place in plan.owners(column * per_column + part):
                    out_ref = out_refs[(shard % plan.pair) ^ core_here]
                    y = (shard // plan.pair) ^ my_y
                    for j in range(plan.n_gy):
                        slot = y * plan.inner + ((j % plan.inner) ^ my_x)
                        z = (j // plan.inner) ^ my_z
                        out_ref[slot, z, place] = lanes[j * plan.cols : (j + 1) * plan.cols]

    for core_here in range(plan.pair):
        pl.when(my_core == core_here)(functools.partial(products, core_here))


def weight_sums(plan, occ, tile, rim, index, grad, n_bx, n_by, rectify, compact):
    size_x, size_y, edge, chans = tile.shape
    smem = pl.BlockSpec(memory_space=pltpu.SMEM)
    anywhere = pl.BlockSpec(memory_space=pl.ANY)
    vmem = pl.BlockSpec(memory_space=pltpu.VMEM)
    voxels = B * B * AMAX * B
    shape = (plan.n_plane, plan.n_z, plan.depth, plan.cols, LANES)
    return pl.pallas_call(
        functools.partial(weight_kernel, plan, n_bx, n_by, index, rectify, compact),
        out_shape=[jax.ShapeDtypeStruct(shape, jnp.bfloat16)] * plan.pair,
        in_specs=[smem] + [anywhere] * 5 + [vmem],
        out_specs=[vmem] * plan.pair,
        scratch_shapes=[
            pltpu.VMEM((size_x + 2, size_y + 2, edge, chans), jnp.bfloat16),
            pltpu.VMEM((3, B + 2, B + 2, AMAX * B, chans), jnp.bfloat16),
            pltpu.VMEM((B, B, AMAX * B, chans), jnp.bfloat16),
            pltpu.VMEM((chans, voxels), jnp.bfloat16),
            pltpu.SemaphoreType.DMA((5,)),
        ],
        compiler_params=pltpu.CompilerParams(vmem_limit_bytes=40 * 1024 * 1024),
        cost_estimate=SMALL,
    )(occ, tile, *rim, grad)


def data_kernel(
    plan, n_bx, n_by, index, gated, n_pieces,
    occ_ref, tile_ref, low_x, high_x, low_y, high_y, *rest,
):
    piece_refs = rest[:n_pieces]
    rest = rest[n_pieces:]
    if gated:
        gate_ref, out_ref, center_ref = rest[:3]
        rest = rest[3:]
    else:
        out_ref = rest[0]
        rest = rest[1:]
    ext_ref, shifted_ref, weight_ref, total_ref, sems = rest
    edge = B
    blocks = pick_blocks(occ_ref, n_bx, n_by)
    my_gx = lax.axis_index("gx")
    my_gy = lax.axis_index("gy")
    if n_pieces == 1:
        for shard in range(plan.n_gx):
            for column in range(plan.n_gy):
                weight_ref[shard, column * plan.cols : (column + 1) * plan.cols] = piece_refs[0][
                    shard * plan.n_gy + column
                ]
    else:
        for piece in range(n_pieces):
            core = piece // plan.n_plane
            slot = piece % plan.n_plane
            shard = my_gx ^ (slot // plan.inner * plan.pair + core)
            for z in range(plan.n_z):
                column = my_gy ^ (z * plan.inner + slot % plan.inner)
                start = pl.multiple_of(column * plan.cols, plan.cols)
                weight_ref[shard, pl.ds(start, plan.cols)] = piece_refs[piece][z]
    load_extended(index, tile_ref, low_x, high_x, low_y, high_y, ext_ref, sems)
    spread_patches(occ_ref, blocks, ext_ref, shifted_ref, n_bx, n_by, False)
    out_ref[...] = jnp.zeros_like(out_ref)

    def kernel_lanes(tile):
        total = None
        for shard, place in plan.owners(tile):
            part = weight_ref[shard, :, place * LANES : (place + 1) * LANES]
            total = part if total is None else total + part
        return total

    halves = plan.chans // LANES
    for column, (shift_x, shift_y) in enumerate(stencil_columns):
        pieces = [window(shifted_ref, 2 - j, 1 - shift_x, 1 - shift_y) for j in range(3)]
        taps = [
            jnp.concatenate(
                [kernel_lanes((3 * column + j) * halves + part) for part in range(halves)], axis=1
            )
            for j in range(3)
        ]
        product = jnp.dot(
            jnp.concatenate(pieces, axis=1),
            jnp.concatenate(taps, axis=0),
            preferred_element_type=jnp.float32,
        )
        if column == 0:
            total_ref[...] = product
        else:
            total_ref[...] += product

    def at_x(x, carry):
        for y in range(edge):
            kept = []
            for index, block in enumerate(blocks):
                start = pl.multiple_of((x * edge + y) * AMAX * edge, AMAX * edge) + index * edge
                value = total_ref[pl.ds(start, edge), :]
                at = (block[0] * edge + x, block[1] * edge + y)
                if gated:
                    value = jnp.where(gate_ref[at].astype(jnp.float32) > 0, value, 0.0)
                    value = jnp.where(block[2] > 0, value, 0.0)
                    kept.append(value)

                @pl.when(block[2] > 0)
                def _():
                    out_ref[at] = value.astype(jnp.bfloat16)

            if gated:
                center_ref[x, y] = jnp.concatenate(kept, axis=0).astype(jnp.bfloat16)
        return carry

    lax.fori_loop(0, edge, at_x, 0)


def data_grad(plan, occ, tile, rim, index, pieces, n_bx, n_by, gate=None):
    size_x, size_y, edge, chans = tile.shape
    smem = pl.BlockSpec(memory_space=pltpu.SMEM)
    anywhere = pl.BlockSpec(memory_space=pl.ANY)
    vmem = pl.BlockSpec(memory_space=pltpu.VMEM)
    voxels = B * B * AMAX * B
    gated = gate is not None
    out_shape = [jax.ShapeDtypeStruct(tile.shape, jnp.bfloat16)]
    if gated:
        out_shape.append(jax.ShapeDtypeStruct((B, B, AMAX * B, chans), jnp.bfloat16))
    return pl.pallas_call(
        functools.partial(data_kernel, plan, n_bx, n_by, index, gated, len(pieces)),
        out_shape=out_shape,
        in_specs=[smem] + [anywhere] * 5 + [vmem] * (len(pieces) + gated),
        out_specs=[vmem] * len(out_shape),
        scratch_shapes=[
            pltpu.VMEM((size_x + 2, size_y + 2, edge, chans), jnp.bfloat16),
            pltpu.VMEM((3, B + 2, B + 2, AMAX * B, chans), jnp.bfloat16),
            pltpu.VMEM((plan.n_gx, chans, plan.depth * LANES), jnp.bfloat16),
            pltpu.VMEM((voxels, chans), jnp.float32),
            pltpu.SemaphoreType.DMA((5,)),
        ],
        compiler_params=pltpu.CompilerParams(vmem_limit_bytes=40 * 1024 * 1024),
        cost_estimate=SMALL,
    )(occ, tile, *rim, *pieces, *([gate] if gated else []))


def after(x, *others):
    return lax.optimization_barrier((x, others))[0]


def first_kernel(
    plan, n_bx, n_by,
    occ_ref, two_ref, one_ref, *rest,
):
    field_refs = rest[:3]
    own_two, own_one, first_x, last_x, first_y, last_y, raw_ref, sems = rest[3:]
    size_x, size_y = field_refs[0].shape[:2]
    copies = []
    for index, ref in enumerate(field_refs):
        for side, strip in enumerate((ref.at[0], ref.at[size_x - 1], ref.at[:, 0], ref.at[:, size_y - 1])):
            size = size_y if side < 2 else size_x
            copies.append(
                pltpu.make_async_copy(
                    strip, raw_ref.at[side, index, pl.ds(0, size)], sems.at[side, index]
                )
            )
    for copy in copies:
        copy.start()
    offset = lax.axis_index("gx") * plan.rows % LANES
    for share_ref, weight_ref in ((own_two, two_ref), (own_one, one_ref)):
        wide = jnp.concatenate(
            [
                weight_ref[...].astype(jnp.float32),
                jnp.zeros((plan.cols, plan.depth * LANES - plan.rows), jnp.float32),
            ],
            axis=1,
        )
        share_ref[...] = pltpu.roll(wide, offset, 1).astype(jnp.bfloat16)
    for copy in copies:
        copy.wait()
    for side, strip_ref in enumerate((first_x, last_x, first_y, last_y)):
        for part in range(n_by if side < 2 else n_bx):
            at = ((0, part), (n_bx - 1, part), (part, 0), (part, n_by - 1))[side]
            rows = slice(part * B, (part + 1) * B)
            for index in range(3):
                value = raw_ref[side, index, rows].astype(jnp.float32)
                if index == 0:
                    value = jnp.maximum(value, 0.0)
                value = jnp.where(occ_ref[at[0], at[1], 0] > 0, value, 0.0)
                strip_ref[index, rows] = value.astype(jnp.bfloat16)


def first_steps(plan, occ, weight_two, weight_one, fields, n_bx, n_by):
    size_x, size_y, edge, chans = fields[0].shape
    smem = pl.BlockSpec(memory_space=pltpu.SMEM)
    anywhere = pl.BlockSpec(memory_space=pl.ANY)
    vmem = pl.BlockSpec(memory_space=pltpu.VMEM)
    share = jax.ShapeDtypeStruct((plan.cols, plan.depth * LANES), jnp.bfloat16)
    along_y = jax.ShapeDtypeStruct((3, size_y, edge, chans), jnp.bfloat16)
    along_x = jax.ShapeDtypeStruct((3, size_x, edge, chans), jnp.bfloat16)
    return pl.pallas_call(
        functools.partial(first_kernel, plan, n_bx, n_by),
        out_shape=[share, share, along_y, along_y, along_x, along_x],
        in_specs=[smem, vmem, vmem] + [anywhere] * 3,
        out_specs=[vmem] * 6,
        scratch_shapes=[
            pltpu.VMEM((4, 3, max(size_x, size_y), edge, chans), jnp.bfloat16),
            pltpu.SemaphoreType.DMA((4, 3)),
        ],
        cost_estimate=SMALL,
    )(occ, weight_two.T, weight_one.T, *fields)


def gather_line(plan, own):
    return jnp.stack([own] + [swap_z(own, plan, slot) for slot in range(1, plan.n_z)])


def gather_plane(plan, line):
    return [line] + [swap_plane(line, plan, slot) for slot in range(1, plan.n_plane)]


def gather_pair(plan, plane):
    return [swap(part, plan, 1, 0) for part in plane] if plan.pair == 2 else []


def reduce_pair(plan, sums):
    total = [sums[0][slot].astype(jnp.float32) for slot in range(plan.n_plane)]
    if plan.pair == 2:
        got = swap(sums[1], plan, 1, 0)
        total = [total[slot] + got[slot].astype(jnp.float32) for slot in range(plan.n_plane)]
    return [total[0]] + [part.astype(jnp.bfloat16) for part in total[1:]]


def swap_parts(plan, parts, swap_one):
    return [swap_one(parts[slot], plan, slot) for slot in range(1, len(parts))]


def reduce_plane(plan, own, got):
    line = own
    for part in got:
        line = line + part.astype(jnp.float32)
    return [line[0]] + [line[slot].astype(jnp.bfloat16) for slot in range(1, plan.n_z)]


def reduce_z(plan, own, got):
    for part in got:
        own = own + part.astype(jnp.float32)
    scale = float(plan.n_gx * plan.n_gy * B**3) ** (-0.5)
    flat = (own * scale).transpose(1, 0, 2).reshape(plan.cols, plan.depth * LANES)
    offset = lax.axis_index("gx") * plan.rows % LANES
    return lax.dynamic_slice(flat, (0, offset), (plan.cols, plan.rows)).T


def ring(axis):
    size = lax.axis_size(axis)
    up = [(i, i + 1) for i in range(size - 1)]
    return up, [(j, i) for i, j in up]


def rims_x(first_x, last_x):
    up, down = ring("gx")
    return lax.ppermute(last_x, "gx", up), lax.ppermute(first_x, "gx", down)


def strips_y(low_x, high_x, first_y, last_y):
    return (
        jnp.concatenate([low_x[:, :1], first_y, high_x[:, :1]], axis=1),
        jnp.concatenate([low_x[:, -1:], last_y, high_x[:, -1:]], axis=1),
    )


def rims_y(first_y, last_y):
    up, down = ring("gy")
    return lax.ppermute(last_y, "gy", up), lax.ppermute(first_y, "gy", down)


def body(inputs, preact, out_grad, weight_one, weight_two, occupancy):
    n_bx, n_by = occupancy.shape[:2]
    plan = Plan(
        lax.axis_size("gx"), lax.axis_size("gy"), weight_one.shape[0], inputs.shape[-1]
    )
    occ = occupancy

    own_two, own_one, first_x, last_x, first_y, last_y = first_steps(
        plan, occ, weight_two, weight_one, (preact, inputs, out_grad), n_bx, n_by
    )
    pieces_one = [lax.all_gather(own_one, BOTH, axis=0)]
    low_x, high_x = rims_x(first_x, last_x)
    sent_y = strips_y(low_x, high_x, first_y, last_y)
    edges = (low_x, high_x) + rims_y(*sent_y)
    line = after(gather_line(plan, own_two), edges)
    sums_two = weight_sums(plan, occ, preact, edges, 0, out_grad, n_bx, n_by, True, False)
    plane = gather_plane(plan, line)
    sums_two = [sums_two[0]] + list(after(sums_two[1:], plane))
    plane_two = reduce_pair(plan, sums_two)
    pieces_two = after(plane + gather_pair(plan, plane), plane_two)
    grad_one, center = data_grad(
        plan, occ, out_grad, edges, 2, pieces_two, n_bx, n_by, preact
    )

    strips = (grad_one[None, 0], grad_one[None, -1], grad_one[None, :, 0], grad_one[None, :, -1])
    center, strips = lax.optimization_barrier((center, strips))
    sums_one = weight_sums(plan, occ, inputs, edges, 1, center, n_bx, n_by, False, True)
    got_two = after(swap_parts(plan, plane_two, swap_plane), sums_one)
    low_x, high_x = after(rims_x(*strips[:2]), sums_one)
    sums_one = [sums_one[0]] + list(after(sums_one[1:], got_two, low_x, high_x))
    edges_one = (low_x, high_x) + rims_y(*strips_y(low_x, high_x, *strips[2:]))
    line_two = reduce_plane(plan, plane_two[0], got_two)
    sums_one = after(sums_one[:1], edges_one, line_two) + sums_one[1:]
    plane_one = reduce_pair(plan, sums_one)
    got = swap_parts(plan, line_two, swap_z)
    grad_one = after(grad_one, plane_one, got)
    (input_grad,) = data_grad(plan, occ, grad_one, edges_one, 0, pieces_one, n_bx, n_by)
    own_two = reduce_z(plan, line_two[0], after(got, input_grad))
    got_one = after(swap_parts(plan, plane_one, swap_plane), input_grad)
    line_one = reduce_plane(plan, plane_one[0], got_one)
    own_one = reduce_z(plan, line_one[0], swap_parts(plan, line_one, swap_z))
    return (input_grad, own_one, own_two)


def solution(mesh):
    return jax.shard_map(
        body,
        mesh=mesh,
        in_specs=(
            P("gx", "gy", None, None),
            P("gx", "gy", None, None),
            P("gx", "gy", None, None),
            P("gx", "gy"),
            P("gx", "gy"),
            P("gx", "gy", None),
        ),
        out_specs=(P("gx", "gy", None, None), P("gx", "gy"), P("gx", "gy")),
        check_vma=False,
    )
```

```python
import functools

import jax
import jax.numpy as jnp
from jax import lax
from jax.experimental import pallas as pl
from jax.experimental.pallas import tpu as pltpu
from jax.sharding import PartitionSpec as P

B = 8
AMAX = 2
LANES = 128
BOTH = ("gx", "gy")
SMALL = pl.CostEstimate(flops=1, bytes_accessed=1, transcendentals=0)

stencil_columns = [(shift_x, shift_y) for shift_x in (-1, 0, 1) for shift_y in (-1, 0, 1)]


class Plan:
    def __init__(self, n_gx, n_gy, rows, chans):
        self.n_gx = n_gx
        self.n_gy = n_gy
        self.rows = rows
        self.chans = chans
        self.cols = chans // n_gy
        self.pair = 2
        self.inner = 2
        self.n_y = n_gx // self.pair
        self.n_z = n_gy // self.inner
        self.n_plane = self.n_y * self.inner
        self.tiles = 27 * chans // LANES
        self.first = [rows * i // LANES for i in range(n_gx)]
        self.offset = [rows * i % LANES for i in range(n_gx)]
        self.depth = max(-(-(self.offset[i] + rows) // LANES) for i in range(n_gx))

    def owners(self, tile):
        return [
            (i, tile - self.first[i])
            for i in range(self.n_gx)
            if tile * LANES < (i + 1) * self.rows and (tile + 1) * LANES > i * self.rows
        ]


def swap(x, plan, flip_gx, flip_gy):
    n_gy = plan.n_gy
    pairs = [
        (i * n_gy + j, (i ^ flip_gx) * n_gy + (j ^ flip_gy))
        for i in range(plan.n_gx)
        for j in range(n_gy)
    ]
    return lax.ppermute(x, BOTH, pairs)


def swap_plane(x, plan, slot):
    return swap(x, plan, slot // plan.inner * plan.pair, slot % plan.inner)


def swap_z(x, plan, slot):
    return swap(x, plan, 0, slot * plan.inner)


def pick_blocks(occ_ref, n_bx, n_by):
    count = jnp.int32(0)
    first = jnp.int32(0)
    second = jnp.int32(0)
    for i in range(n_bx * n_by):
        on = occ_ref[i // n_by, i % n_by, 0] > 0
        first = jnp.where(jnp.logical_and(on, count == 0), i, first)
        second = jnp.where(jnp.logical_and(on, count == 1), i, second)
        count = count + on.astype(jnp.int32)
    blocks = []
    for slot, index in enumerate((first, second)):
        blocks.append((index // n_by, index % n_by, (count > slot).astype(jnp.int32)))
    return blocks


def block_mask(occ_ref, block, step_x, step_y, n_bx, n_by):
    bx = block[0] + step_x
    by = block[1] + step_y
    inside = (bx >= 0) & (bx < n_bx) & (by >= 0) & (by < n_by)
    near = occ_ref[jnp.clip(bx, 0, n_bx - 1), jnp.clip(by, 0, n_by - 1), 0]
    return jnp.where(inside, near, 1) * block[2]


def extended_copies(index, tile_ref, low_x, high_x, low_y, high_y, ext_ref, sems):
    size_x, size_y = tile_ref.shape[:2]
    return [
        pltpu.make_async_copy(
            tile_ref, ext_ref.at[pl.ds(1, size_x), pl.ds(1, size_y)], sems.at[0]
        ),
        pltpu.make_async_copy(low_x.at[index], ext_ref.at[0, pl.ds(1, size_y)], sems.at[1]),
        pltpu.make_async_copy(
            high_x.at[index], ext_ref.at[size_x + 1, pl.ds(1, size_y)], sems.at[2]
        ),
        pltpu.make_async_copy(low_y.at[index], ext_ref.at[:, 0], sems.at[3]),
        pltpu.make_async_copy(high_y.at[index], ext_ref.at[:, size_y + 1], sems.at[4]),
    ]


def load_extended(*refs):
    copies = extended_copies(*refs)
    for copy in copies:
        copy.start()
    for copy in copies:
        copy.wait()


def spread_patches(occ_ref, blocks, ext_ref, shifted_ref, n_bx, n_by):
    edge = B
    row = lax.broadcasted_iota(jnp.int32, (edge, ext_ref.shape[-1]), 0)

    def at_x(x, carry):
        step_x = jnp.where(x == 0, -1, jnp.where(x == edge + 1, 1, 0))
        masks = [
            [block_mask(occ_ref, block, step_x, step_y, n_bx, n_by) > 0 for step_y in (-1, 0, 1)]
            for block in blocks
        ]
        for y in range(edge + 2):
            side = 0 if y == 0 else (2 if y == edge + 1 else 1)
            planes = [[], [], []]
            for index, block in enumerate(blocks):
                value = ext_ref[block[0] * edge + x, block[1] * edge + y].astype(jnp.float32)
                value = jnp.where(masks[index][side], value, 0.0)
                below = jnp.where(row == 0, 0.0, pltpu.roll(value, 1, 0))
                above = jnp.where(row == edge - 1, 0.0, pltpu.roll(value, edge - 1, 0))
                for plane, part in zip(planes, (below, value, above)):
                    plane.append(part)
            for j in range(3):
                shifted_ref[j, x, y] = jnp.concatenate(planes[j], axis=0).astype(jnp.bfloat16)
        return carry

    lax.fori_loop(0, edge + 2, at_x, 0)


def spread_rows(patch_ref, put):
    edge = B
    row = lax.broadcasted_iota(jnp.int32, (AMAX * edge, patch_ref.shape[-1]), 0) % edge

    def at_x(x, carry):
        for y in range(edge + 2):
            kept = patch_ref[x, y]
            value = kept.astype(jnp.float32)
            below = jnp.where(row == 0, 0.0, pltpu.roll(value, 1, 0))
            above = jnp.where(row == edge - 1, 0.0, pltpu.roll(value, AMAX * edge - 1, 0))
            put(0, x, y, below.astype(jnp.bfloat16))
            put(1, x, y, kept)
            put(2, x, y, above.astype(jnp.bfloat16))
        return carry

    lax.fori_loop(0, edge + 2, at_x, 0)


def patch_kernel(n_bx, n_by, occ_ref, *rest):
    tile_refs = rest[:3]
    low_x, high_x, low_y, high_y = rest[3:7]
    patches_ref, ext_ref, sems = rest[7:]
    edge = B
    blocks = pick_blocks(occ_ref, n_bx, n_by)
    copies = []
    for index, tile_ref in enumerate(tile_refs):
        copies.append(
            extended_copies(
                index, tile_ref, low_x, high_x, low_y, high_y, ext_ref.at[index], sems.at[index]
            )
        )
    for group in copies:
        for copy in group:
            copy.start()
    for index in range(len(tile_refs)):
        for copy in copies[index]:
            copy.wait()

        def at_x(x, carry, index=index):
            step_x = jnp.where(x == 0, -1, jnp.where(x == edge + 1, 1, 0))
            masks = [
                [
                    block_mask(occ_ref, block, step_x, step_y, n_bx, n_by) > 0
                    for step_y in (-1, 0, 1)
                ]
                for block in blocks
            ]
            for y in range(edge + 2):
                side = 0 if y == 0 else (2 if y == edge + 1 else 1)
                parts = []
                for slot, block in enumerate(blocks):
                    value = ext_ref[index, block[0] * edge + x, block[1] * edge + y]
                    value = value.astype(jnp.float32)
                    if index == 0:
                        value = jnp.maximum(value, 0.0)
                    parts.append(jnp.where(masks[slot][side], value, 0.0))
                patches_ref[index, x, y] = jnp.concatenate(parts, axis=0).astype(jnp.bfloat16)
            return carry

        lax.fori_loop(0, edge + 2, at_x, 0)


def patches_of(occ, fields, edges, n_bx, n_by):
    size_x, size_y, edge, chans = fields[0].shape
    anywhere = pl.BlockSpec(memory_space=pl.ANY)
    vmem = pl.BlockSpec(memory_space=pltpu.VMEM)
    shape = (len(fields), B + 2, B + 2, AMAX * B, chans)
    return pl.pallas_call(
        functools.partial(patch_kernel, n_bx, n_by),
        out_shape=jax.ShapeDtypeStruct(shape, jnp.bfloat16),
        in_specs=[pl.BlockSpec(memory_space=pltpu.SMEM)] + [anywhere] * 7,
        out_specs=vmem,
        scratch_shapes=[
            pltpu.VMEM((3, size_x + 2, size_y + 2, edge, chans), jnp.bfloat16),
            pltpu.SemaphoreType.DMA((3, 5)),
        ],
        compiler_params=pltpu.CompilerParams(vmem_limit_bytes=40 * 1024 * 1024),
        cost_estimate=SMALL,
    )(occ, *fields, *edges)


def window(shifted_ref, plane, start_x, start_y, lanes=slice(None)):
    edge = B
    piece = shifted_ref[plane, start_x : start_x + edge, start_y : start_y + edge, :, lanes]
    return piece.reshape(edge * edge * AMAX * edge, piece.shape[-1])


def weight_kernel(plan, field, own_ref, other_ref, *rest):
    *center_refs, out_ref, shifted_ref, turned_ref = rest
    voxels = B * B * AMAX * B
    pair = (own_ref, other_ref)
    for index, patch_ref in enumerate(pair):

        def put(j, x, y, rows, index=index):
            shifted_ref[index, j, x, y] = rows

        spread_rows(patch_ref.at[field], put)
        if center_refs:
            center = center_refs[index][...]
        else:
            center = patch_ref[2, 1 : B + 1, 1 : B + 1]
        turned = center.reshape(voxels, plan.chans).astype(jnp.float32).T
        turned_ref[:, index * voxels : (index + 1) * voxels] = turned.astype(jnp.bfloat16)
    my_gx = lax.axis_index("gx")
    my_gy = lax.axis_index("gy")
    my_core = my_gx % plan.pair
    my_y = my_gx // plan.pair
    my_x = my_gy % plan.inner
    my_z = my_gy // plan.inner
    halves = plan.chans // LANES

    def taps(tile):
        column, j = divmod(tile // halves, 3)
        shift_x, shift_y = stencil_columns[column]
        lanes = slice(tile % halves * LANES, (tile % halves + 1) * LANES)
        return jnp.concatenate(
            [
                window(shifted_ref.at[index], j, 1 + shift_x, 1 + shift_y, lanes)
                for index in range(len(pair))
            ],
            axis=0,
        )

    def products(core_here):
        places = []
        for tile in range(plan.tiles):
            mine = [owner for owner in plan.owners(tile) if owner[0] % plan.pair == core_here]
            if mine:
                places.append((tile, mine))
        at_once = 6
        for begin in range(0, len(places), at_once):
            group = places[begin : begin + at_once]
            product = jnp.dot(
                turned_ref[...],
                jnp.concatenate([taps(tile) for tile, _ in group], axis=1),
                preferred_element_type=jnp.float32,
            ).astype(jnp.bfloat16)
            for part, (_, mine) in enumerate(group):
                lanes = product[:, part * LANES : (part + 1) * LANES]
                for shard, place in mine:
                    y = (shard // plan.pair) ^ my_y
                    for j in range(plan.n_gy):
                        slot = y * plan.inner + ((j % plan.inner) ^ my_x)
                        z = (j // plan.inner) ^ my_z
                        out_ref[slot, z, place] = lanes[j * plan.cols : (j + 1) * plan.cols]

    for core_here in range(plan.pair):
        pl.when(my_core == core_here)(functools.partial(products, core_here))


def weight_sums(plan, field, own, other, centers=()):
    chans = plan.chans
    vmem = pl.BlockSpec(memory_space=pltpu.VMEM)
    voxels = B * B * AMAX * B
    shape = (plan.n_plane, plan.n_z, plan.depth, plan.cols, LANES)
    return pl.pallas_call(
        functools.partial(weight_kernel, plan, field),
        out_shape=jax.ShapeDtypeStruct(shape, jnp.bfloat16),
        in_specs=[vmem] * (2 + len(centers)),
        out_specs=vmem,
        scratch_shapes=[
            pltpu.VMEM((plan.pair, 3, B + 2, B + 2, AMAX * B, chans), jnp.bfloat16),
            pltpu.VMEM((chans, plan.pair * voxels), jnp.bfloat16),
        ],
        compiler_params=pltpu.CompilerParams(vmem_limit_bytes=40 * 1024 * 1024),
        cost_estimate=SMALL,
    )(own, other, *centers)


def data_kernel(plan, n_bx, n_by, n_sources, gated, distances, occ_ref, *rest):
    source_refs = rest[:n_sources]
    rest = rest[n_sources:]
    piece_refs = rest[: len(distances)]
    rest = rest[len(distances) :]
    if gated:
        gate_ref, out_ref, center_ref = rest[:3]
        rest = rest[3:]
    else:
        out_ref = rest[0]
        rest = rest[1:]
    ext_ref, shifted_ref, weight_ref, total_ref, sems = rest
    edge = B
    blocks = pick_blocks(occ_ref, n_bx, n_by)
    my_gx = lax.axis_index("gx")
    my_gy = lax.axis_index("gy")
    for piece_ref, flips in zip(piece_refs, distances):
        for place, (flip_gx, flip_gy) in enumerate(flips):
            start = pl.multiple_of((my_gy ^ flip_gy) * plan.cols, plan.cols)
            weight_ref[my_gx ^ flip_gx, pl.ds(start, plan.cols)] = piece_ref[place]
    if n_sources == 1:

        def put(j, x, y, rows):
            shifted_ref[j, x, y] = rows

        spread_rows(source_refs[0].at[2], put)
    else:
        load_extended(0, *source_refs, ext_ref, sems)
        spread_patches(occ_ref, blocks, ext_ref, shifted_ref, n_bx, n_by)
    out_ref[...] = jnp.zeros_like(out_ref)

    def kernel_lanes(tile):
        total = None
        for shard, place in plan.owners(tile):
            part = weight_ref[shard, :, place * LANES : (place + 1) * LANES]
            total = part if total is None else total + part
        return total

    halves = plan.chans // LANES
    for column, (shift_x, shift_y) in enumerate(stencil_columns):
        pieces = [window(shifted_ref, 2 - j, 1 - shift_x, 1 - shift_y) for j in range(3)]
        taps = [
            jnp.concatenate(
                [kernel_lanes((3 * column + j) * halves + part) for part in range(halves)], axis=1
            )
            for j in range(3)
        ]
        product = jnp.dot(
            jnp.concatenate(pieces, axis=1),
            jnp.concatenate(taps, axis=0),
            preferred_element_type=jnp.float32,
        )
        if column == 0:
            total_ref[...] = product
        else:
            total_ref[...] += product

    def at_x(x, carry):
        for y in range(edge):
            kept = []
            for index, block in enumerate(blocks):
                start = pl.multiple_of((x * edge + y) * AMAX * edge, AMAX * edge) + index * edge
                value = total_ref[pl.ds(start, edge), :]
                at = (block[0] * edge + x, block[1] * edge + y)
                if gated:
                    value = jnp.where(gate_ref[at].astype(jnp.float32) > 0, value, 0.0)
                    value = jnp.where(block[2] > 0, value, 0.0)
                    kept.append(value)

                @pl.when(block[2] > 0)
                def _():
                    out_ref[at] = value.astype(jnp.bfloat16)

            if gated:
                center_ref[x, y] = jnp.concatenate(kept, axis=0).astype(jnp.bfloat16)
        return carry

    lax.fori_loop(0, edge, at_x, 0)


def data_grad(plan, occ, shape, sources, pieces, distances, n_bx, n_by, gate=None):
    size_x, size_y, edge, chans = shape
    smem = pl.BlockSpec(memory_space=pltpu.SMEM)
    vmem = pl.BlockSpec(memory_space=pltpu.VMEM)
    source = vmem if len(sources) == 1 else pl.BlockSpec(memory_space=pl.ANY)
    voxels = B * B * AMAX * B
    gated = gate is not None
    out_shape = [jax.ShapeDtypeStruct(shape, jnp.bfloat16)]
    if gated:
        out_shape.append(jax.ShapeDtypeStruct((B, B, AMAX * B, chans), jnp.bfloat16))
    return pl.pallas_call(
        functools.partial(data_kernel, plan, n_bx, n_by, len(sources), gated, distances),
        out_shape=out_shape,
        in_specs=[smem] + [source] * len(sources) + [vmem] * (len(pieces) + gated),
        out_specs=[vmem] * len(out_shape),
        scratch_shapes=[
            pltpu.VMEM((size_x + 2, size_y + 2, edge, chans), jnp.bfloat16),
            pltpu.VMEM((3, B + 2, B + 2, AMAX * B, chans), jnp.bfloat16),
            pltpu.VMEM((plan.n_gx, chans, plan.depth * LANES), jnp.bfloat16),
            pltpu.VMEM((voxels, chans), jnp.float32),
            pltpu.SemaphoreType.DMA((5,)),
        ],
        compiler_params=pltpu.CompilerParams(vmem_limit_bytes=40 * 1024 * 1024),
        cost_estimate=SMALL,
    )(occ, *sources, *pieces, *([gate] if gated else []))


def after(x, *others):
    return lax.optimization_barrier((x, others))[0]


def first_kernel(
    plan, n_bx, n_by,
    occ_ref, two_ref, one_ref, *rest,
):
    field_refs = rest[:3]
    own_two, own_one, first_x, last_x, first_y, last_y, raw_ref, sems = rest[3:]
    size_x, size_y = field_refs[0].shape[:2]
    copies = []
    for index, ref in enumerate(field_refs):
        for side, strip in enumerate((ref.at[0], ref.at[size_x - 1], ref.at[:, 0], ref.at[:, size_y - 1])):
            size = size_y if side < 2 else size_x
            copies.append(
                pltpu.make_async_copy(
                    strip, raw_ref.at[side, index, pl.ds(0, size)], sems.at[side, index]
                )
            )
    for copy in copies:
        copy.start()
    offset = lax.axis_index("gx") * plan.rows % LANES
    for share_ref, weight_ref in ((own_two, two_ref), (own_one, one_ref)):
        wide = jnp.concatenate(
            [
                weight_ref[...].astype(jnp.float32),
                jnp.zeros((plan.cols, plan.depth * LANES - plan.rows), jnp.float32),
            ],
            axis=1,
        )
        share_ref[...] = pltpu.roll(wide, offset, 1).astype(jnp.bfloat16)
    for copy in copies:
        copy.wait()
    for side, strip_ref in enumerate((first_x, last_x, first_y, last_y)):
        for part in range(n_by if side < 2 else n_bx):
            at = ((0, part), (n_bx - 1, part), (part, 0), (part, n_by - 1))[side]
            rows = slice(part * B, (part + 1) * B)
            for index in range(3):
                value = raw_ref[side, index, rows].astype(jnp.float32)
                if index == 0:
                    value = jnp.maximum(value, 0.0)
                value = jnp.where(occ_ref[at[0], at[1], 0] > 0, value, 0.0)
                strip_ref[index, rows] = value.astype(jnp.bfloat16)


def first_steps(plan, occ, weight_two, weight_one, fields, n_bx, n_by):
    size_x, size_y, edge, chans = fields[0].shape
    smem = pl.BlockSpec(memory_space=pltpu.SMEM)
    anywhere = pl.BlockSpec(memory_space=pl.ANY)
    vmem = pl.BlockSpec(memory_space=pltpu.VMEM)
    share = jax.ShapeDtypeStruct((plan.cols, plan.depth * LANES), jnp.bfloat16)
    along_y = jax.ShapeDtypeStruct((3, size_y, edge, chans), jnp.bfloat16)
    along_x = jax.ShapeDtypeStruct((3, size_x, edge, chans), jnp.bfloat16)
    return pl.pallas_call(
        functools.partial(first_kernel, plan, n_bx, n_by),
        out_shape=[share, share, along_y, along_y, along_x, along_x],
        in_specs=[smem, vmem, vmem] + [anywhere] * 3,
        out_specs=[vmem] * 6,
        scratch_shapes=[
            pltpu.VMEM((4, 3, max(size_x, size_y), edge, chans), jnp.bfloat16),
            pltpu.SemaphoreType.DMA((4, 3)),
        ],
        cost_estimate=SMALL,
    )(occ, weight_two.T, weight_one.T, *fields)


class Gathered:
    def __init__(self, array, distances):
        self.array = array
        self.distances = distances

    def from_others(self, plan, flips):
        return [
            Gathered(
                swap(self.array, plan, flip_gx, flip_gy),
                [(i ^ flip_gx, j ^ flip_gy) for i, j in self.distances],
            )
            for flip_gx, flip_gy in flips
        ]

    def joined(self, others):
        parts = [self] + others
        return Gathered(
            jnp.concatenate([part.array for part in parts], axis=0),
            [distance for part in parts for distance in part.distances],
        )

    def part(self, start, stop):
        return Gathered(self.array[start:stop], self.distances[start:stop])

    def after(self, *others):
        return Gathered(after(self.array, *others), self.distances)


def plane_flips(plan):
    return [
        (slot // plan.inner * plan.pair, slot % plan.inner) for slot in range(1, plan.n_plane)
    ]


def z_steps(plan):
    step = plan.n_z // 2
    while step > 0:
        yield [(0, step * plan.inner)]
        step //= 2


def both_cores(plan, gathered):
    return [gathered] + gathered.from_others(plan, [(1, 0)])


class Halving:
    def __init__(self, plan, sums):
        self.plan = plan
        bits = [1 << i for i in range(plan.n_plane.bit_length() - 1)]
        self.orders = [bits, bits[1:] + bits[:1]]
        half = plan.n_z // 2
        self.slots = [list(range(plan.n_plane))] * 2
        self.parts = [sums[:, :half], sums[:, half:]]
        self.step = 0

    def sends(self):
        out = []
        for half in range(2):
            bit = self.orders[half][self.step]
            away = [i for i, slot in enumerate(self.slots[half]) if slot & bit]
            out.append(take(self.parts[half], away).astype(jnp.bfloat16))
        return out

    def swaps(self, sends):
        out = []
        for half in range(2):
            slot = self.orders[half][self.step]
            plan = self.plan
            out.append(
                swap(sends[half], plan, slot // plan.inner * plan.pair, slot % plan.inner)
            )
        return out

    def add(self, got):
        for half in range(2):
            bit = self.orders[half][self.step]
            stay = [i for i, slot in enumerate(self.slots[half]) if not slot & bit]
            kept = take(self.parts[half], stay).astype(jnp.float32)
            self.parts[half] = kept + got[half].astype(jnp.float32)
            self.slots = list(self.slots)
            self.slots[half] = [self.slots[half][i] for i in stay]
        self.step += 1

    def done(self):
        return self.step == len(self.orders[0])

    def line(self):
        return jnp.concatenate([part[0] for part in self.parts], axis=0)


def take(array, indices):
    return jnp.concatenate([array[i : i + 1] for i in indices], axis=0)


def halve_z_step(plan, line):
    step = line.shape[0] // 2
    got = swap_z(line[step:].astype(jnp.bfloat16), plan, step)
    return line[:step].astype(jnp.float32) + got.astype(jnp.float32)


def spread_z(plan, line, *before):
    got = [
        swap_z(line[slot].astype(jnp.bfloat16), plan, slot) for slot in range(1, plan.n_z)
    ]
    own = line[0]
    for part in after(got, *before):
        own = own + part.astype(jnp.float32)
    return own


def finished(plan, own):
    scale = float(plan.n_gx * plan.n_gy * B**3) ** (-0.5)
    flat = (own * scale).transpose(1, 0, 2).reshape(plan.cols, plan.depth * LANES)
    offset = lax.axis_index("gx") * plan.rows % LANES
    return lax.dynamic_slice(flat, (0, offset), (plan.cols, plan.rows)).T


def ring(axis):
    size = lax.axis_size(axis)
    up = [(i, i + 1) for i in range(size - 1)]
    return up, [(j, i) for i, j in up]


def rims_x(first_x, last_x):
    up, down = ring("gx")
    return lax.ppermute(last_x, "gx", up), lax.ppermute(first_x, "gx", down)


def strips_y(low_x, high_x, first_y, last_y):
    return (
        jnp.concatenate([low_x[:, :1], first_y, high_x[:, :1]], axis=1),
        jnp.concatenate([low_x[:, -1:], last_y, high_x[:, -1:]], axis=1),
    )


def rims_y(first_y, last_y):
    up, down = ring("gy")
    return lax.ppermute(last_y, "gy", up), lax.ppermute(first_y, "gy", down)


def body(inputs, preact, out_grad, weight_one, weight_two, occupancy):
    n_bx, n_by = occupancy.shape[:2]
    plan = Plan(
        lax.axis_size("gx"), lax.axis_size("gy"), weight_one.shape[0], inputs.shape[-1]
    )
    occ = occupancy

    own_two, own_one, first_x, last_x, first_y, last_y = first_steps(
        plan, occ, weight_two, weight_one, (preact, inputs, out_grad), n_bx, n_by
    )
    low_x, high_x = rims_x(first_x, last_x)
    steps = list(z_steps(plan))
    two = Gathered(own_two[None], [(0, 0)])
    for flips in steps[:-1]:
        two = two.joined(two.from_others(plan, flips))
    sent_y = after(strips_y(low_x, high_x, first_y, last_y), two.array)
    for flips in steps[-1:]:
        two = two.joined(two.from_others(plan, flips))
    one = Gathered(own_one[None], [(0, 0)]).after(low_x, high_x)
    one = one.joined(one.from_others(plan, plane_flips(plan)))
    edges = after((low_x, high_x) + rims_y(*sent_y), one.array, two.array)
    two = two.after(edges)
    patches = patches_of(occ, (preact, inputs, out_grad), edges, n_bx, n_by)
    other = swap(patches, plan, 1, 0)
    sums_two = weight_sums(plan, 0, patches, other)
    for flips in steps[:-1]:
        one = one.joined([part.after(sums_two) for part in one.from_others(plan, flips)])
    others = two.from_others(plan, plane_flips(plan))
    two = two.joined([part.after(sums_two) for part in others]).after(one.array)
    halving_two = Halving(plan, sums_two)
    sends = after(halving_two.sends(), two.array)
    got_two = halving_two.swaps(sends)
    pieces = both_cores(plan, two)
    grad_one, center = data_grad(
        plan, occ, inputs.shape, [patches], after([part.array for part in pieces], sends),
        [part.distances for part in pieces], n_bx, n_by, preact,
    )
    other_center = swap(center, plan, 1, 0)
    halving_two.add(after(got_two, grad_one))
    while not halving_two.done():
        sends = halving_two.sends()
        got_two = halving_two.swaps(sends)
        if halving_two.step + 1 == len(halving_two.orders[0]):
            sums_one = weight_sums(plan, 1, patches, other, (after(center, sends), other_center))
            got_two = after(got_two, sums_one)
        halving_two.add(got_two)
    for flips in steps[-1:]:
        others = one.after(two.array).from_others(plan, flips)
        one = one.joined([part.after(sums_one) for part in others])
    line_two = halving_two.line()

    halving_one = Halving(plan, after(sums_one, got_two))
    sends = halving_one.sends()
    got_one = halving_one.swaps(sends)
    line_two = halve_z_step(plan, after(line_two, sends))
    strips = (grad_one[None, 0], grad_one[None, -1], grad_one[None, :, 0], grad_one[None, :, -1])
    strips = after(strips, sends)
    low_x, high_x = rims_x(*strips[:2])
    sent_y = strips_y(low_x, high_x, *strips[2:])
    halving_one.add(after(got_one, sent_y))
    while not halving_one.done():
        sends = halving_one.sends()
        got_one = halving_one.swaps(sends)
        if halving_one.step + 1 == len(halving_one.orders[0]):
            edges_one = (low_x, high_x) + rims_y(*after(sent_y, sends))
            line_two = after(line_two, sends)
            while line_two.shape[0] > 1:
                line_two = halve_z_step(plan, line_two)
            got_one = after(got_one, edges_one)
        halving_one.add(got_one)
    line_one = halving_one.line()
    pieces = both_cores(plan, one)
    (input_grad,) = data_grad(
        plan, occ, inputs.shape, (after(grad_one, line_one),) + edges_one,
        [part.array for part in pieces], [part.distances for part in pieces], n_bx, n_by,
    )
    own_one = spread_z(plan, line_one, input_grad)
    return (input_grad, finished(plan, own_one), finished(plan, line_two[0]))


def solution(mesh):
    return jax.shard_map(
        body,
        mesh=mesh,
        in_specs=(
            P("gx", "gy", None, None),
            P("gx", "gy", None, None),
            P("gx", "gy", None, None),
            P("gx", "gy"),
            P("gx", "gy"),
            P("gx", "gy", None),
        ),
        out_specs=(P("gx", "gy", None, None), P("gx", "gy"), P("gx", "gy")),
        check_vma=False,
    )
```

```python
import functools

import jax
import jax.numpy as jnp
from jax import lax
from jax.experimental import pallas as pl
from jax.experimental.pallas import tpu as pltpu
from jax.sharding import PartitionSpec as P

B = 8
AMAX = 2
LANES = 128
BOTH = ("gx", "gy")
SMALL = pl.CostEstimate(flops=1, bytes_accessed=1, transcendentals=0)

stencil_columns = [(shift_x, shift_y) for shift_x in (-1, 0, 1) for shift_y in (-1, 0, 1)]


class Plan:
    def __init__(self, n_gx, n_gy, rows, chans):
        self.n_gx = n_gx
        self.n_gy = n_gy
        self.rows = rows
        self.chans = chans
        self.cols = chans // n_gy
        self.pair = 2
        self.inner = 2
        self.n_y = n_gx // self.pair
        self.n_z = n_gy // self.inner
        self.n_plane = self.n_y * self.inner
        self.tiles = 27 * chans // LANES
        self.first = [rows * i // LANES for i in range(n_gx)]
        self.offset = [rows * i % LANES for i in range(n_gx)]
        self.depth = max(-(-(self.offset[i] + rows) // LANES) for i in range(n_gx))

    def owners(self, tile):
        return [
            (i, tile - self.first[i])
            for i in range(self.n_gx)
            if tile * LANES < (i + 1) * self.rows and (tile + 1) * LANES > i * self.rows
        ]


def swap(x, plan, flip_gx, flip_gy):
    n_gy = plan.n_gy
    pairs = [
        (i * n_gy + j, (i ^ flip_gx) * n_gy + (j ^ flip_gy))
        for i in range(plan.n_gx)
        for j in range(n_gy)
    ]
    return lax.ppermute(x, BOTH, pairs)


def swap_plane(x, plan, slot):
    return swap(x, plan, slot // plan.inner * plan.pair, slot % plan.inner)


def swap_z(x, plan, slot):
    return swap(x, plan, 0, slot * plan.inner)


def pick_blocks(occ_ref, n_bx, n_by):
    count = jnp.int32(0)
    first = jnp.int32(0)
    second = jnp.int32(0)
    for i in range(n_bx * n_by):
        on = occ_ref[i // n_by, 0, i % n_by] > 0
        first = jnp.where(jnp.logical_and(on, count == 0), i, first)
        second = jnp.where(jnp.logical_and(on, count == 1), i, second)
        count = count + on.astype(jnp.int32)
    blocks = []
    for slot, index in enumerate((first, second)):
        blocks.append((index // n_by, index % n_by, (count > slot).astype(jnp.int32)))
    return blocks


def block_mask(occ_ref, block, step_x, step_y, n_bx, n_by):
    bx = block[0] + step_x
    by = block[1] + step_y
    inside = (bx >= 0) & (bx < n_bx) & (by >= 0) & (by < n_by)
    near = occ_ref[jnp.clip(bx, 0, n_bx - 1), 0, jnp.clip(by, 0, n_by - 1)]
    return jnp.where(inside, near, 1) * block[2]


def extended_copies(index, tile_ref, low_x, high_x, low_y, high_y, ext_ref, sems):
    size_x, size_y = tile_ref.shape[:2]
    return [
        pltpu.make_async_copy(
            tile_ref, ext_ref.at[pl.ds(1, size_x), pl.ds(1, size_y)], sems.at[0]
        ),
        pltpu.make_async_copy(low_x.at[index], ext_ref.at[0, pl.ds(1, size_y)], sems.at[1]),
        pltpu.make_async_copy(
            high_x.at[index], ext_ref.at[size_x + 1, pl.ds(1, size_y)], sems.at[2]
        ),
        pltpu.make_async_copy(low_y.at[index], ext_ref.at[:, 0], sems.at[3]),
        pltpu.make_async_copy(high_y.at[index], ext_ref.at[:, size_y + 1], sems.at[4]),
    ]


def spread_patches(occ_ref, blocks, ext_ref, shifted_ref, n_bx, n_by):
    edge = B
    row = lax.broadcasted_iota(jnp.int32, (edge, ext_ref.shape[-1]), 0)

    def at_x(x, carry):
        step_x = jnp.where(x == 0, -1, jnp.where(x == edge + 1, 1, 0))
        masks = [
            [block_mask(occ_ref, block, step_x, step_y, n_bx, n_by) > 0 for step_y in (-1, 0, 1)]
            for block in blocks
        ]
        for y in range(edge + 2):
            side = 0 if y == 0 else (2 if y == edge + 1 else 1)
            planes = [[], [], []]
            for index, block in enumerate(blocks):
                value = ext_ref[block[0] * edge + x, block[1] * edge + y].astype(jnp.float32)
                value = jnp.where(masks[index][side], value, 0.0)
                below = jnp.where(row == 0, 0.0, pltpu.roll(value, 1, 0))
                above = jnp.where(row == edge - 1, 0.0, pltpu.roll(value, edge - 1, 0))
                for plane, part in zip(planes, (below, value, above)):
                    plane.append(part)
            for j in range(3):
                shifted_ref[j, x, y] = jnp.concatenate(planes[j], axis=0).astype(jnp.bfloat16)
        return carry

    lax.fori_loop(0, edge + 2, at_x, 0)


def spread_rows(patch_ref, put):
    edge = B
    row = lax.broadcasted_iota(jnp.int32, (AMAX * edge, patch_ref.shape[-1]), 0) % edge

    def at_x(x, carry):
        for y in range(edge + 2):
            kept = patch_ref[x, y]
            value = kept.astype(jnp.float32)
            below = jnp.where(row == 0, 0.0, pltpu.roll(value, 1, 0))
            above = jnp.where(row == edge - 1, 0.0, pltpu.roll(value, AMAX * edge - 1, 0))
            put(0, x, y, below.astype(jnp.bfloat16))
            put(1, x, y, kept)
            put(2, x, y, above.astype(jnp.bfloat16))
        return carry

    lax.fori_loop(0, edge + 2, at_x, 0)


def patch_kernel(n_bx, n_by, occ_ref, *rest):
    tile_refs = rest[:3]
    low_x, high_x, low_y, high_y = rest[3:7]
    patches_ref, ext_ref, sems = rest[7:]
    edge = B
    blocks = pick_blocks(occ_ref, n_bx, n_by)
    copies = []
    for index, tile_ref in enumerate(tile_refs):
        copies.append(
            extended_copies(
                index, tile_ref, low_x, high_x, low_y, high_y, ext_ref.at[index], sems.at[index]
            )
        )
    for group in copies:
        for copy in group:
            copy.start()
    for index in range(len(tile_refs)):
        for copy in copies[index]:
            copy.wait()

        def at_x(x, carry, index=index):
            step_x = jnp.where(x == 0, -1, jnp.where(x == edge + 1, 1, 0))
            masks = [
                [
                    block_mask(occ_ref, block, step_x, step_y, n_bx, n_by) > 0
                    for step_y in (-1, 0, 1)
                ]
                for block in blocks
            ]
            for y in range(edge + 2):
                side = 0 if y == 0 else (2 if y == edge + 1 else 1)
                parts = []
                for slot, block in enumerate(blocks):
                    value = ext_ref[index, block[0] * edge + x, block[1] * edge + y]
                    value = value.astype(jnp.float32)
                    if index == 0:
                        value = jnp.maximum(value, 0.0)
                    parts.append(jnp.where(masks[slot][side], value, 0.0))
                patches_ref[index, x, y] = jnp.concatenate(parts, axis=0).astype(jnp.bfloat16)
            return carry

        lax.fori_loop(0, edge + 2, at_x, 0)


def patches_of(occ, fields, edges, n_bx, n_by):
    size_x, size_y, edge, chans = fields[0].shape
    anywhere = pl.BlockSpec(memory_space=pl.ANY)
    vmem = pl.BlockSpec(memory_space=pltpu.VMEM)
    shape = (len(fields), B + 2, B + 2, AMAX * B, chans)
    return pl.pallas_call(
        functools.partial(patch_kernel, n_bx, n_by),
        out_shape=jax.ShapeDtypeStruct(shape, jnp.bfloat16),
        in_specs=[pl.BlockSpec(memory_space=pltpu.SMEM)] + [anywhere] * 7,
        out_specs=vmem,
        scratch_shapes=[
            pltpu.VMEM((3, size_x + 2, size_y + 2, edge, chans), jnp.bfloat16),
            pltpu.SemaphoreType.DMA((3, 5)),
        ],
        compiler_params=pltpu.CompilerParams(vmem_limit_bytes=40 * 1024 * 1024),
        cost_estimate=SMALL,
    )(occ, *fields, *edges)


def window(shifted_ref, plane, start_x, start_y, lanes=slice(None)):
    edge = B
    piece = shifted_ref[plane, start_x : start_x + edge, start_y : start_y + edge, :, lanes]
    return piece.reshape(edge * edge * AMAX * edge, piece.shape[-1])


def weight_kernel(plan, field, own_ref, other_ref, *rest):
    *center_refs, out_ref, shifted_ref, turned_ref = rest
    voxels = B * B * AMAX * B
    pair = (own_ref, other_ref)
    for index, patch_ref in enumerate(pair):

        def put(j, x, y, rows, index=index):
            shifted_ref[index, j, x, y] = rows

        spread_rows(patch_ref.at[field], put)
        if center_refs:
            center = center_refs[index][...]
        else:
            center = patch_ref[2, 1 : B + 1, 1 : B + 1]
        turned = center.reshape(voxels, plan.chans).astype(jnp.float32).T
        turned_ref[:, index * voxels : (index + 1) * voxels] = turned.astype(jnp.bfloat16)
    my_gx = lax.axis_index("gx")
    my_gy = lax.axis_index("gy")
    my_core = my_gx % plan.pair
    my_y = my_gx // plan.pair
    my_x = my_gy % plan.inner
    my_z = my_gy // plan.inner
    halves = plan.chans // LANES

    def taps(tile):
        column, j = divmod(tile // halves, 3)
        shift_x, shift_y = stencil_columns[column]
        lanes = slice(tile % halves * LANES, (tile % halves + 1) * LANES)
        return jnp.concatenate(
            [
                window(shifted_ref.at[index], j, 1 + shift_x, 1 + shift_y, lanes)
                for index in range(len(pair))
            ],
            axis=0,
        )

    def products(core_here):
        places = []
        for tile in range(plan.tiles):
            mine = [owner for owner in plan.owners(tile) if owner[0] % plan.pair == core_here]
            if mine:
                places.append((tile, mine))
        at_once = 6
        for begin in range(0, len(places), at_once):
            group = places[begin : begin + at_once]
            product = jnp.dot(
                turned_ref[...],
                jnp.concatenate([taps(tile) for tile, _ in group], axis=1),
                preferred_element_type=jnp.float32,
            ).astype(jnp.bfloat16)
            for part, (_, mine) in enumerate(group):
                lanes = product[:, part * LANES : (part + 1) * LANES]
                for shard, place in mine:
                    y = (shard // plan.pair) ^ my_y
                    for j in range(plan.n_gy):
                        slot = y * plan.inner + ((j % plan.inner) ^ my_x)
                        z = (j // plan.inner) ^ my_z
                        out_ref[slot, z, place] = lanes[j * plan.cols : (j + 1) * plan.cols]

    for core_here in range(plan.pair):
        pl.when(my_core == core_here)(functools.partial(products, core_here))


def weight_sums(plan, field, own, other, centers=()):
    chans = plan.chans
    vmem = pl.BlockSpec(memory_space=pltpu.VMEM)
    voxels = B * B * AMAX * B
    shape = (plan.n_plane, plan.n_z, plan.depth, plan.cols, LANES)
    return pl.pallas_call(
        functools.partial(weight_kernel, plan, field),
        out_shape=jax.ShapeDtypeStruct(shape, jnp.bfloat16),
        in_specs=[vmem] * (2 + len(centers)),
        out_specs=vmem,
        scratch_shapes=[
            pltpu.VMEM((plan.pair, 3, B + 2, B + 2, AMAX * B, chans), jnp.bfloat16),
            pltpu.VMEM((chans, plan.pair * voxels), jnp.bfloat16),
        ],
        compiler_params=pltpu.CompilerParams(vmem_limit_bytes=40 * 1024 * 1024),
        cost_estimate=SMALL,
    )(own, other, *centers)


def data_kernel(plan, n_bx, n_by, n_sources, gated, distances, occ_ref, *rest):
    source_refs = rest[:n_sources]
    rest = rest[n_sources:]
    piece_refs = rest[: len(distances)]
    rest = rest[len(distances) :]
    if gated:
        gate_ref, out_ref, center_ref = rest[:3]
        rest = rest[3:]
    else:
        out_ref = rest[0]
        rest = rest[1:]
    ext_ref, shifted_ref, weight_ref, total_ref, sems = rest
    edge = B
    blocks = pick_blocks(occ_ref, n_bx, n_by)
    my_gx = lax.axis_index("gx")
    my_gy = lax.axis_index("gy")
    copies = [] if n_sources == 1 else extended_copies(0, *source_refs, ext_ref, sems)
    for copy in copies:
        copy.start()
    for piece_ref, flips in zip(piece_refs, distances):
        for place, (flip_gx, flip_gy) in enumerate(flips):
            start = pl.multiple_of((my_gy ^ flip_gy) * plan.cols, plan.cols)
            weight_ref[my_gx ^ flip_gx, pl.ds(start, plan.cols)] = piece_ref[place]
    out_ref[...] = jnp.zeros_like(out_ref)
    for copy in copies:
        copy.wait()
    if n_sources == 1:

        def put(j, x, y, rows):
            shifted_ref[j, x, y] = rows

        spread_rows(source_refs[0].at[2], put)
    else:
        spread_patches(occ_ref, blocks, ext_ref, shifted_ref, n_bx, n_by)

    def kernel_lanes(tile):
        total = None
        for shard, place in plan.owners(tile):
            part = weight_ref[shard, :, place * LANES : (place + 1) * LANES]
            total = part if total is None else total + part
        return total

    halves = plan.chans // LANES
    for column, (shift_x, shift_y) in enumerate(stencil_columns):
        pieces = [window(shifted_ref, 2 - j, 1 - shift_x, 1 - shift_y) for j in range(3)]
        taps = [
            jnp.concatenate(
                [kernel_lanes((3 * column + j) * halves + part) for part in range(halves)], axis=1
            )
            for j in range(3)
        ]
        product = jnp.dot(
            jnp.concatenate(pieces, axis=1),
            jnp.concatenate(taps, axis=0),
            preferred_element_type=jnp.float32,
        )
        if column == 0:
            total_ref[...] = product
        else:
            total_ref[...] += product

    def at_x(x, carry):
        for y in range(edge):
            kept = []
            for index, block in enumerate(blocks):
                start = pl.multiple_of((x * edge + y) * AMAX * edge, AMAX * edge) + index * edge
                value = total_ref[pl.ds(start, edge), :]
                at = (block[0] * edge + x, block[1] * edge + y)
                if gated:
                    value = jnp.where(gate_ref[at].astype(jnp.float32) > 0, value, 0.0)
                    value = jnp.where(block[2] > 0, value, 0.0)
                    kept.append(value)

                @pl.when(block[2] > 0)
                def _():
                    out_ref[at] = value.astype(jnp.bfloat16)

            if gated:
                center_ref[x, y] = jnp.concatenate(kept, axis=0).astype(jnp.bfloat16)
        return carry

    lax.fori_loop(0, edge, at_x, 0)


def data_grad(plan, occ, shape, sources, pieces, distances, n_bx, n_by, gate=None):
    size_x, size_y, edge, chans = shape
    smem = pl.BlockSpec(memory_space=pltpu.SMEM)
    vmem = pl.BlockSpec(memory_space=pltpu.VMEM)
    source = vmem if len(sources) == 1 else pl.BlockSpec(memory_space=pl.ANY)
    voxels = B * B * AMAX * B
    gated = gate is not None
    out_shape = [jax.ShapeDtypeStruct(shape, jnp.bfloat16)]
    if gated:
        out_shape.append(jax.ShapeDtypeStruct((B, B, AMAX * B, chans), jnp.bfloat16))
    return pl.pallas_call(
        functools.partial(data_kernel, plan, n_bx, n_by, len(sources), gated, distances),
        out_shape=out_shape,
        in_specs=[smem] + [source] * len(sources) + [vmem] * (len(pieces) + gated),
        out_specs=[vmem] * len(out_shape),
        scratch_shapes=[
            pltpu.VMEM((size_x + 2, size_y + 2, edge, chans), jnp.bfloat16),
            pltpu.VMEM((3, B + 2, B + 2, AMAX * B, chans), jnp.bfloat16),
            pltpu.VMEM((plan.n_gx, chans, plan.depth * LANES), jnp.bfloat16),
            pltpu.VMEM((voxels, chans), jnp.float32),
            pltpu.SemaphoreType.DMA((5,)),
        ],
        compiler_params=pltpu.CompilerParams(vmem_limit_bytes=40 * 1024 * 1024),
        cost_estimate=SMALL,
    )(occ, *sources, *pieces, *([gate] if gated else []))


def after(x, *others):
    return lax.optimization_barrier((x, others))[0]


def first_kernel(
    plan, n_bx, n_by,
    occ_ref, two_ref, one_ref, *rest,
):
    field_refs = rest[:3]
    own_two, own_one, first_x, last_x, first_y, last_y, raw_ref, sems = rest[3:]
    size_x, size_y = field_refs[0].shape[:2]
    copies = []
    for index, ref in enumerate(field_refs):
        for side, strip in enumerate((ref.at[0], ref.at[size_x - 1], ref.at[:, 0], ref.at[:, size_y - 1])):
            size = size_y if side < 2 else size_x
            copies.append(
                pltpu.make_async_copy(
                    strip, raw_ref.at[side, index, pl.ds(0, size)], sems.at[side, index]
                )
            )
    for copy in copies:
        copy.start()
    offset = lax.axis_index("gx") * plan.rows % LANES
    for share_ref, weight_ref in ((own_two, two_ref), (own_one, one_ref)):
        wide = jnp.concatenate(
            [
                weight_ref[...].astype(jnp.float32),
                jnp.zeros((plan.cols, plan.depth * LANES - plan.rows), jnp.float32),
            ],
            axis=1,
        )
        share_ref[...] = pltpu.roll(wide, offset, 1).astype(jnp.bfloat16)
    for copy in copies:
        copy.wait()
    for side, strip_ref in enumerate((first_x, last_x, first_y, last_y)):
        for part in range(n_by if side < 2 else n_bx):
            at = ((0, part), (n_bx - 1, part), (part, 0), (part, n_by - 1))[side]
            rows = slice(part * B, (part + 1) * B)
            for index in range(3):
                value = raw_ref[side, index, rows].astype(jnp.float32)
                if index == 0:
                    value = jnp.maximum(value, 0.0)
                value = jnp.where(occ_ref[at[0], 0, at[1]] > 0, value, 0.0)
                strip_ref[index, rows] = value.astype(jnp.bfloat16)


def first_steps(plan, occ, weight_two, weight_one, fields, n_bx, n_by):
    size_x, size_y, edge, chans = fields[0].shape
    smem = pl.BlockSpec(memory_space=pltpu.SMEM)
    anywhere = pl.BlockSpec(memory_space=pl.ANY)
    vmem = pl.BlockSpec(memory_space=pltpu.VMEM)
    share = jax.ShapeDtypeStruct((plan.cols, plan.depth * LANES), jnp.bfloat16)
    along_y = jax.ShapeDtypeStruct((3, size_y, edge, chans), jnp.bfloat16)
    along_x = jax.ShapeDtypeStruct((3, size_x, edge, chans), jnp.bfloat16)
    return pl.pallas_call(
        functools.partial(first_kernel, plan, n_bx, n_by),
        out_shape=[share, share, along_y, along_y, along_x, along_x],
        in_specs=[smem, vmem, vmem] + [anywhere] * 3,
        out_specs=[vmem] * 6,
        scratch_shapes=[
            pltpu.VMEM((4, 3, max(size_x, size_y), edge, chans), jnp.bfloat16),
            pltpu.SemaphoreType.DMA((4, 3)),
        ],
        cost_estimate=SMALL,
    )(occ, weight_two.T, weight_one.T, *fields)


class Gathered:
    def __init__(self, array, distances):
        self.array = array
        self.distances = distances

    def from_others(self, plan, flips):
        return [
            Gathered(
                swap(self.array, plan, flip_gx, flip_gy),
                [(i ^ flip_gx, j ^ flip_gy) for i, j in self.distances],
            )
            for flip_gx, flip_gy in flips
        ]

    def joined(self, others):
        parts = [self] + others
        return Gathered(
            jnp.concatenate([part.array for part in parts], axis=0),
            [distance for part in parts for distance in part.distances],
        )

    def part(self, start, stop):
        return Gathered(self.array[start:stop], self.distances[start:stop])

    def after(self, *others):
        return Gathered(after(self.array, *others), self.distances)


def plane_flips(plan):
    return [
        (slot // plan.inner * plan.pair, slot % plan.inner) for slot in range(1, plan.n_plane)
    ]


def z_steps(plan):
    step = plan.n_z // 2
    while step > 0:
        yield [(0, step * plan.inner)]
        step //= 2


def both_cores(plan, gathered):
    return [gathered] + gathered.from_others(plan, [(1, 0)])


class Halving:
    def __init__(self, plan, sums):
        self.plan = plan
        bits = [1 << i for i in range(plan.n_plane.bit_length() - 1)]
        self.orders = [bits, bits[1:] + bits[:1]]
        half = plan.n_z // 2
        self.slots = [list(range(plan.n_plane))] * 2
        self.parts = [sums[:, :half], sums[:, half:]]
        self.step = 0

    def sends(self):
        out = []
        for half in range(2):
            bit = self.orders[half][self.step]
            away = [i for i, slot in enumerate(self.slots[half]) if slot & bit]
            out.append(take(self.parts[half], away).astype(jnp.bfloat16))
        return out

    def swaps(self, sends):
        out = []
        for half in range(2):
            slot = self.orders[half][self.step]
            plan = self.plan
            out.append(
                swap(sends[half], plan, slot // plan.inner * plan.pair, slot % plan.inner)
            )
        return out

    def add(self, got):
        for half in range(2):
            bit = self.orders[half][self.step]
            stay = [i for i, slot in enumerate(self.slots[half]) if not slot & bit]
            kept = take(self.parts[half], stay).astype(jnp.float32)
            self.parts[half] = kept + got[half].astype(jnp.float32)
            self.slots = list(self.slots)
            self.slots[half] = [self.slots[half][i] for i in stay]
        self.step += 1

    def last(self):
        return self.step + 1 == len(self.orders[0])

    def done(self):
        return self.step == len(self.orders[0])

    def line(self):
        return jnp.concatenate([part[0] for part in self.parts], axis=0)


def take(array, indices):
    return jnp.concatenate([array[i : i + 1] for i in indices], axis=0)


def halve_z_step(plan, line, step):
    got = swap_z(line[1::2].astype(jnp.bfloat16), plan, step)
    return line[0::2].astype(jnp.float32) + got.astype(jnp.float32)


def spread_z(plan, line, *before):
    got = [
        swap_z(line[slot].astype(jnp.bfloat16), plan, slot) for slot in range(1, plan.n_z)
    ]
    own = line[0]
    for part in after(got, *before):
        own = own + part.astype(jnp.float32)
    return own


def finished(plan, own):
    scale = float(plan.n_gx * plan.n_gy * B**3) ** (-0.5)
    flat = (own * scale).transpose(1, 0, 2).reshape(plan.cols, plan.depth * LANES)
    offset = lax.axis_index("gx") * plan.rows % LANES
    return lax.dynamic_slice(flat, (0, offset), (plan.cols, plan.rows)).T


def ring(axis):
    size = lax.axis_size(axis)
    up = [(i, i + 1) for i in range(size - 1)]
    return up, [(j, i) for i, j in up]


def rims_x(first_x, last_x):
    up, down = ring("gx")
    return lax.ppermute(last_x, "gx", up), lax.ppermute(first_x, "gx", down)


def strips_y(low_x, high_x, first_y, last_y):
    return (
        jnp.concatenate([low_x[:, :1], first_y, high_x[:, :1]], axis=1),
        jnp.concatenate([low_x[:, -1:], last_y, high_x[:, -1:]], axis=1),
    )


def rims_y(first_y, last_y):
    up, down = ring("gy")
    return lax.ppermute(last_y, "gy", up), lax.ppermute(first_y, "gy", down)


def body(inputs, preact, out_grad, weight_one, weight_two, occupancy):
    n_bx, n_by = occupancy.shape[:2]
    plan = Plan(
        lax.axis_size("gx"), lax.axis_size("gy"), weight_one.shape[0], inputs.shape[-1]
    )
    occ = occupancy.transpose(0, 2, 1)

    own_two, own_one, first_x, last_x, first_y, last_y = first_steps(
        plan, occ, weight_two, weight_one, (preact, inputs, out_grad), n_bx, n_by
    )
    low_x, high_x = rims_x(first_x, last_x)
    steps = list(z_steps(plan))
    two = Gathered(own_two[None], [(0, 0)])
    for flips in steps[:-1]:
        two = two.joined(two.from_others(plan, flips))
    sent_y = after(strips_y(low_x, high_x, first_y, last_y), two.array)
    for flips in steps[-1:]:
        two = two.joined(two.from_others(plan, flips))
    one = Gathered(own_one[None], [(0, 0)]).after(sent_y)
    one = one.joined(one.from_others(plan, plane_flips(plan)))
    edges = after((low_x, high_x) + rims_y(*sent_y), one.array, two.array)
    two = two.after(edges)
    patches = patches_of(occ, (preact, inputs, out_grad), edges, n_bx, n_by)
    other = swap(patches, plan, 1, 0)
    sums_two = weight_sums(plan, 0, patches, other)
    for flips in steps[:-1]:
        one = one.joined([part.after(sums_two) for part in one.from_others(plan, flips)])
    others = two.from_others(plan, plane_flips(plan))
    two = two.joined([part.after(sums_two) for part in others]).after(one.array)
    halving_two = Halving(plan, sums_two)
    sends = after(halving_two.sends(), two.array)
    got_two = halving_two.swaps(sends)
    pieces = both_cores(plan, two)
    grad_one, center = data_grad(
        plan, occ, inputs.shape, [patches], after([part.array for part in pieces], sends),
        [part.distances for part in pieces], n_bx, n_by, preact,
    )
    other_center = swap(center, plan, 1, 0)
    halving_two.add(after(got_two, grad_one))
    while not halving_two.done():
        sends = halving_two.sends()
        got_two = halving_two.swaps(sends)
        if halving_two.last():
            sums_one = weight_sums(plan, 1, patches, other, (after(center, sends), other_center))
            got_two = after(got_two, sums_one)
        halving_two.add(got_two)
    for flips in steps[-1:]:
        others = one.after(two.array).from_others(plan, flips)
        one = one.joined([part.after(sums_one) for part in others])
    line_two = halving_two.line()

    halving_one = Halving(plan, after(sums_one, got_two))
    sends = halving_one.sends()
    got_one = halving_one.swaps(sends)
    line_two = halve_z_step(plan, after(line_two, sends), 1)
    strips = (grad_one[None, 0], grad_one[None, -1], grad_one[None, :, 0], grad_one[None, :, -1])
    strips = after(strips, sends)
    low_x, high_x = rims_x(*strips[:2])
    sent_y = strips_y(low_x, high_x, *strips[2:])
    halving_one.add(after(got_one, sent_y))
    while not halving_one.done():
        sends = halving_one.sends()
        got_one = halving_one.swaps(sends)
        if halving_one.last():
            line_two = after(line_two, sends)
            while line_two.shape[0] > 1:
                line_two = halve_z_step(plan, line_two, plan.n_z // line_two.shape[0])
            edges_one = (low_x, high_x) + rims_y(*after(sent_y, sends))
            got_one = after(got_one)
        halving_one.add(got_one)
    line_one = halving_one.line()
    pieces = both_cores(plan, one)
    (input_grad,) = data_grad(
        plan, occ, inputs.shape, (after(grad_one, line_one),) + edges_one,
        [part.array for part in pieces], [part.distances for part in pieces], n_bx, n_by,
    )
    own_one = spread_z(plan, line_one, input_grad)
    return (input_grad, finished(plan, own_one), finished(plan, line_two[0]))


def solution(mesh):
    return jax.shard_map(
        body,
        mesh=mesh,
        in_specs=(
            P("gx", "gy", None, None),
            P("gx", "gy", None, None),
            P("gx", "gy", None, None),
            P("gx", "gy"),
            P("gx", "gy"),
            P("gx", "gy", None),
        ),
        out_specs=(P("gx", "gy", None, None), P("gx", "gy"), P("gx", "gy")),
        check_vma=False,
    )
```

```python
import functools

import jax
import jax.numpy as jnp
from jax import lax
from jax.experimental import pallas as pl
from jax.experimental.pallas import tpu as pltpu
from jax.sharding import PartitionSpec as P

B = 8
AMAX = 2
LANES = 128
BOTH = ("gx", "gy")
SMALL = pl.CostEstimate(flops=1, bytes_accessed=1, transcendentals=0)

stencil_columns = [(shift_x, shift_y) for shift_x in (-1, 0, 1) for shift_y in (-1, 0, 1)]


class Plan:
    def __init__(self, n_gx, n_gy, rows, chans):
        self.n_gx = n_gx
        self.n_gy = n_gy
        self.rows = rows
        self.chans = chans
        self.cols = chans // n_gy
        self.pair = 2
        self.inner = 2
        self.n_y = n_gx // self.pair
        self.n_z = n_gy // self.inner
        self.n_plane = self.n_y * self.inner
        self.tiles = 27 * chans // LANES
        self.first = [rows * i // LANES for i in range(n_gx)]
        self.offset = [rows * i % LANES for i in range(n_gx)]
        self.depth = max(-(-(self.offset[i] + rows) // LANES) for i in range(n_gx))

    def owners(self, tile):
        return [
            (i, tile - self.first[i])
            for i in range(self.n_gx)
            if tile * LANES < (i + 1) * self.rows and (tile + 1) * LANES > i * self.rows
        ]


def swap(x, plan, flip_gx, flip_gy):
    n_gy = plan.n_gy
    pairs = [
        (i * n_gy + j, (i ^ flip_gx) * n_gy + (j ^ flip_gy))
        for i in range(plan.n_gx)
        for j in range(n_gy)
    ]
    return lax.ppermute(x, BOTH, pairs)


def swap_plane(x, plan, slot):
    return swap(x, plan, slot // plan.inner * plan.pair, slot % plan.inner)


def swap_z(x, plan, slot):
    return swap(x, plan, 0, slot * plan.inner)


def pick_blocks(occ_ref, n_bx, n_by):
    count = jnp.int32(0)
    first = jnp.int32(0)
    second = jnp.int32(0)
    for i in range(n_bx * n_by):
        on = occ_ref[i // n_by, 0, i % n_by] > 0
        first = jnp.where(jnp.logical_and(on, count == 0), i, first)
        second = jnp.where(jnp.logical_and(on, count == 1), i, second)
        count = count + on.astype(jnp.int32)
    blocks = []
    for slot, index in enumerate((first, second)):
        blocks.append((index // n_by, index % n_by, (count > slot).astype(jnp.int32)))
    return blocks


def block_mask(occ_ref, block, step_x, step_y, n_bx, n_by):
    bx = block[0] + step_x
    by = block[1] + step_y
    inside = (bx >= 0) & (bx < n_bx) & (by >= 0) & (by < n_by)
    near = occ_ref[jnp.clip(bx, 0, n_bx - 1), 0, jnp.clip(by, 0, n_by - 1)]
    return jnp.where(inside, near, 1) * block[2]


def extended_copies(index, tile_ref, low_x, high_x, low_y, high_y, ext_ref, sems):
    size_x, size_y = tile_ref.shape[:2]
    return [
        pltpu.make_async_copy(
            tile_ref, ext_ref.at[pl.ds(1, size_x), pl.ds(1, size_y)], sems.at[0]
        ),
        pltpu.make_async_copy(low_x.at[index], ext_ref.at[0, pl.ds(1, size_y)], sems.at[1]),
        pltpu.make_async_copy(
            high_x.at[index], ext_ref.at[size_x + 1, pl.ds(1, size_y)], sems.at[2]
        ),
        pltpu.make_async_copy(low_y.at[index], ext_ref.at[:, 0], sems.at[3]),
        pltpu.make_async_copy(high_y.at[index], ext_ref.at[:, size_y + 1], sems.at[4]),
    ]


def spread_patches(occ_ref, blocks, ext_ref, shifted_ref, n_bx, n_by):
    edge = B
    row = lax.broadcasted_iota(jnp.int32, (edge, ext_ref.shape[-1]), 0)

    def at_x(x, carry):
        step_x = jnp.where(x == 0, -1, jnp.where(x == edge + 1, 1, 0))
        masks = [
            [block_mask(occ_ref, block, step_x, step_y, n_bx, n_by) > 0 for step_y in (-1, 0, 1)]
            for block in blocks
        ]
        for y in range(edge + 2):
            side = 0 if y == 0 else (2 if y == edge + 1 else 1)
            planes = [[], [], []]
            for index, block in enumerate(blocks):
                value = ext_ref[block[0] * edge + x, block[1] * edge + y].astype(jnp.float32)
                value = jnp.where(masks[index][side], value, 0.0)
                below = jnp.where(row == 0, 0.0, pltpu.roll(value, 1, 0))
                above = jnp.where(row == edge - 1, 0.0, pltpu.roll(value, edge - 1, 0))
                for plane, part in zip(planes, (below, value, above)):
                    plane.append(part)
            for j in range(3):
                shifted_ref[j, x, y] = jnp.concatenate(planes[j], axis=0).astype(jnp.bfloat16)
        return carry

    lax.fori_loop(0, edge + 2, at_x, 0)


def spread_rows(patch_ref, put):
    edge = B
    row = lax.broadcasted_iota(jnp.int32, (AMAX * edge, patch_ref.shape[-1]), 0) % edge

    def at_x(x, carry):
        for y in range(edge + 2):
            kept = patch_ref[x, y]
            value = kept.astype(jnp.float32)
            below = jnp.where(row == 0, 0.0, pltpu.roll(value, 1, 0))
            above = jnp.where(row == edge - 1, 0.0, pltpu.roll(value, AMAX * edge - 1, 0))
            put(0, x, y, below.astype(jnp.bfloat16))
            put(1, x, y, kept)
            put(2, x, y, above.astype(jnp.bfloat16))
        return carry

    lax.fori_loop(0, edge + 2, at_x, 0)


def patch_kernel(n_bx, n_by, occ_ref, *rest):
    tile_refs = rest[:3]
    low_x, high_x, low_y, high_y = rest[3:7]
    patches_ref, ext_ref, sems = rest[7:]
    edge = B
    blocks = pick_blocks(occ_ref, n_bx, n_by)
    copies = []
    for index, tile_ref in enumerate(tile_refs):
        copies.append(
            extended_copies(
                index, tile_ref, low_x, high_x, low_y, high_y, ext_ref.at[index], sems.at[index]
            )
        )
    for group in copies:
        for copy in group:
            copy.start()
    for index in range(len(tile_refs)):
        for copy in copies[index]:
            copy.wait()

        def at_x(x, carry, index=index):
            step_x = jnp.where(x == 0, -1, jnp.where(x == edge + 1, 1, 0))
            masks = [
                [
                    block_mask(occ_ref, block, step_x, step_y, n_bx, n_by) > 0
                    for step_y in (-1, 0, 1)
                ]
                for block in blocks
            ]
            for y in range(edge + 2):
                side = 0 if y == 0 else (2 if y == edge + 1 else 1)
                parts = []
                for slot, block in enumerate(blocks):
                    value = ext_ref[index, block[0] * edge + x, block[1] * edge + y]
                    value = value.astype(jnp.float32)
                    if index == 0:
                        value = jnp.maximum(value, 0.0)
                    parts.append(jnp.where(masks[slot][side], value, 0.0))
                patches_ref[index, x, y] = jnp.concatenate(parts, axis=0).astype(jnp.bfloat16)
            return carry

        lax.fori_loop(0, edge + 2, at_x, 0)


def patches_of(occ, fields, edges, n_bx, n_by):
    size_x, size_y, edge, chans = fields[0].shape
    anywhere = pl.BlockSpec(memory_space=pl.ANY)
    vmem = pl.BlockSpec(memory_space=pltpu.VMEM)
    shape = (len(fields), B + 2, B + 2, AMAX * B, chans)
    return pl.pallas_call(
        functools.partial(patch_kernel, n_bx, n_by),
        out_shape=jax.ShapeDtypeStruct(shape, jnp.bfloat16),
        in_specs=[pl.BlockSpec(memory_space=pltpu.SMEM)] + [anywhere] * 7,
        out_specs=vmem,
        scratch_shapes=[
            pltpu.VMEM((3, size_x + 2, size_y + 2, edge, chans), jnp.bfloat16),
            pltpu.SemaphoreType.DMA((3, 5)),
        ],
        compiler_params=pltpu.CompilerParams(vmem_limit_bytes=40 * 1024 * 1024),
        cost_estimate=SMALL,
    )(occ, *fields, *edges)


def window(shifted_ref, plane, start_x, start_y, lanes=slice(None)):
    edge = B
    piece = shifted_ref[plane, start_x : start_x + edge, start_y : start_y + edge, :, lanes]
    return piece.reshape(edge * edge * AMAX * edge, piece.shape[-1])


def weight_kernel(plan, field, own_ref, other_ref, *rest):
    *center_refs, out_ref, shifted_ref, turned_ref = rest
    voxels = B * B * AMAX * B
    pair = (own_ref, other_ref)
    for index, patch_ref in enumerate(pair):

        def put(j, x, y, rows, index=index):
            shifted_ref[index, j, x, y] = rows

        spread_rows(patch_ref.at[field], put)
        if center_refs:
            center = center_refs[index][...]
        else:
            center = patch_ref[2, 1 : B + 1, 1 : B + 1]
        turned = center.reshape(voxels, plan.chans).astype(jnp.float32).T
        turned_ref[:, index * voxels : (index + 1) * voxels] = turned.astype(jnp.bfloat16)
    my_gx = lax.axis_index("gx")
    my_gy = lax.axis_index("gy")
    my_core = my_gx % plan.pair
    my_y = my_gx // plan.pair
    my_x = my_gy % plan.inner
    my_z = my_gy // plan.inner
    halves = plan.chans // LANES

    def taps(tile):
        column, j = divmod(tile // halves, 3)
        shift_x, shift_y = stencil_columns[column]
        lanes = slice(tile % halves * LANES, (tile % halves + 1) * LANES)
        return jnp.concatenate(
            [
                window(shifted_ref.at[index], j, 1 + shift_x, 1 + shift_y, lanes)
                for index in range(len(pair))
            ],
            axis=0,
        )

    def products(core_here):
        places = []
        for tile in range(plan.tiles):
            mine = [owner for owner in plan.owners(tile) if owner[0] % plan.pair == core_here]
            if mine:
                places.append((tile, mine))
        at_once = 6
        for begin in range(0, len(places), at_once):
            group = places[begin : begin + at_once]
            product = jnp.dot(
                turned_ref[...],
                jnp.concatenate([taps(tile) for tile, _ in group], axis=1),
                preferred_element_type=jnp.float32,
            ).astype(jnp.bfloat16)
            for part, (_, mine) in enumerate(group):
                lanes = product[:, part * LANES : (part + 1) * LANES]
                for shard, place in mine:
                    y = (shard // plan.pair) ^ my_y
                    for j in range(plan.n_gy):
                        slot = y * plan.inner + ((j % plan.inner) ^ my_x)
                        z = (j // plan.inner) ^ my_z
                        out_ref[slot, z, place] = lanes[j * plan.cols : (j + 1) * plan.cols]

    for core_here in range(plan.pair):
        pl.when(my_core == core_here)(functools.partial(products, core_here))


def weight_sums(plan, field, own, other, centers=()):
    chans = plan.chans
    vmem = pl.BlockSpec(memory_space=pltpu.VMEM)
    voxels = B * B * AMAX * B
    shape = (plan.n_plane, plan.n_z, plan.depth, plan.cols, LANES)
    return pl.pallas_call(
        functools.partial(weight_kernel, plan, field),
        out_shape=jax.ShapeDtypeStruct(shape, jnp.bfloat16),
        in_specs=[vmem] * (2 + len(centers)),
        out_specs=vmem,
        scratch_shapes=[
            pltpu.VMEM((plan.pair, 3, B + 2, B + 2, AMAX * B, chans), jnp.bfloat16),
            pltpu.VMEM((chans, plan.pair * voxels), jnp.bfloat16),
        ],
        compiler_params=pltpu.CompilerParams(vmem_limit_bytes=40 * 1024 * 1024),
        cost_estimate=SMALL,
    )(own, other, *centers)


def data_kernel(plan, n_bx, n_by, n_sources, gated, distances, occ_ref, *rest):
    source_refs = rest[:n_sources]
    rest = rest[n_sources:]
    piece_refs = rest[: len(distances)]
    rest = rest[len(distances) :]
    if gated:
        gate_ref, out_ref, center_ref = rest[:3]
        rest = rest[3:]
    else:
        out_ref = rest[0]
        rest = rest[1:]
    ext_ref, shifted_ref, weight_ref, total_ref, sems, weight_sems = rest
    edge = B
    blocks = pick_blocks(occ_ref, n_bx, n_by)
    my_gx = lax.axis_index("gx")
    my_gy = lax.axis_index("gy")
    copies = [] if n_sources == 1 else extended_copies(0, *source_refs, ext_ref, sems)
    for copy in copies:
        copy.start()
    late = []
    for piece, (piece_ref, flips) in enumerate(zip(piece_refs, distances)):
        for place, (flip_gx, flip_gy) in enumerate(flips):
            start = pl.multiple_of((my_gy ^ flip_gy) * plan.cols, plan.cols)
            rows = weight_ref.at[my_gx ^ flip_gx, pl.ds(start, plan.cols)]
            if not gated and piece == 1:
                copy = pltpu.make_async_copy(piece_ref.at[place], rows, weight_sems.at[place])
                copy.start()
                late.append(copy)
            else:
                rows[...] = piece_ref[place]
    out_ref[...] = jnp.zeros_like(out_ref)
    for copy in copies:
        copy.wait()
    if n_sources == 1:

        def put(j, x, y, rows):
            shifted_ref[j, x, y] = rows

        spread_rows(source_refs[0].at[2], put)
    else:
        spread_patches(occ_ref, blocks, ext_ref, shifted_ref, n_bx, n_by)
    for copy in late:
        copy.wait()

    def kernel_lanes(tile):
        total = None
        for shard, place in plan.owners(tile):
            part = weight_ref[shard, :, place * LANES : (place + 1) * LANES]
            total = part if total is None else total + part
        return total

    halves = plan.chans // LANES
    for column, (shift_x, shift_y) in enumerate(stencil_columns):
        pieces = [window(shifted_ref, 2 - j, 1 - shift_x, 1 - shift_y) for j in range(3)]
        taps = [
            jnp.concatenate(
                [kernel_lanes((3 * column + j) * halves + part) for part in range(halves)], axis=1
            )
            for j in range(3)
        ]
        product = jnp.dot(
            jnp.concatenate(pieces, axis=1),
            jnp.concatenate(taps, axis=0),
            preferred_element_type=jnp.float32,
        )
        if column == 0:
            total_ref[...] = product
        else:
            total_ref[...] += product

    def at_x(x, carry):
        for y in range(edge):
            kept = []
            for index, block in enumerate(blocks):
                start = pl.multiple_of((x * edge + y) * AMAX * edge, AMAX * edge) + index * edge
                value = total_ref[pl.ds(start, edge), :]
                at = (block[0] * edge + x, block[1] * edge + y)
                if gated:
                    value = jnp.where(gate_ref[at].astype(jnp.float32) > 0, value, 0.0)
                    value = jnp.where(block[2] > 0, value, 0.0)
                    kept.append(value)

                @pl.when(block[2] > 0)
                def _():
                    out_ref[at] = value.astype(jnp.bfloat16)

            if gated:
                center_ref[x, y] = jnp.concatenate(kept, axis=0).astype(jnp.bfloat16)
        return carry

    lax.fori_loop(0, edge, at_x, 0)


def data_grad(plan, occ, shape, sources, pieces, distances, n_bx, n_by, gate=None):
    size_x, size_y, edge, chans = shape
    smem = pl.BlockSpec(memory_space=pltpu.SMEM)
    vmem = pl.BlockSpec(memory_space=pltpu.VMEM)
    anywhere = pl.BlockSpec(memory_space=pl.ANY)
    source = vmem if len(sources) == 1 else anywhere
    voxels = B * B * AMAX * B
    gated = gate is not None
    out_shape = [jax.ShapeDtypeStruct(shape, jnp.bfloat16)]
    if gated:
        out_shape.append(jax.ShapeDtypeStruct((B, B, AMAX * B, chans), jnp.bfloat16))
    return pl.pallas_call(
        functools.partial(data_kernel, plan, n_bx, n_by, len(sources), gated, distances),
        out_shape=out_shape,
        in_specs=[smem] + [source] * len(sources) + [vmem, vmem if gated else anywhere] + [vmem] * gated,
        out_specs=[vmem] * len(out_shape),
        scratch_shapes=[
            pltpu.VMEM((size_x + 2, size_y + 2, edge, chans), jnp.bfloat16),
            pltpu.VMEM((3, B + 2, B + 2, AMAX * B, chans), jnp.bfloat16),
            pltpu.VMEM((plan.n_gx, chans, plan.depth * LANES), jnp.bfloat16),
            pltpu.VMEM((voxels, chans), jnp.float32),
            pltpu.SemaphoreType.DMA((5,)),
            pltpu.SemaphoreType.DMA((len(distances[1]),)),
        ],
        compiler_params=pltpu.CompilerParams(vmem_limit_bytes=40 * 1024 * 1024),
        cost_estimate=SMALL,
    )(occ, *sources, *pieces, *([gate] if gated else []))


def after(x, *others):
    return lax.optimization_barrier((x, others))[0]


def first_kernel(
    plan, n_bx, n_by,
    occ_ref, two_ref, one_ref, *rest,
):
    field_refs = rest[:3]
    own_two, own_one, first_x, last_x, first_y, last_y, raw_ref, sems = rest[3:]
    size_x, size_y = field_refs[0].shape[:2]
    copies = []
    for index, ref in enumerate(field_refs):
        for side, strip in enumerate((ref.at[0], ref.at[size_x - 1], ref.at[:, 0], ref.at[:, size_y - 1])):
            size = size_y if side < 2 else size_x
            copies.append(
                pltpu.make_async_copy(
                    strip, raw_ref.at[side, index, pl.ds(0, size)], sems.at[side, index]
                )
            )
    for copy in copies:
        copy.start()
    offset = lax.axis_index("gx") * plan.rows % LANES
    for share_ref, weight_ref in ((own_two, two_ref), (own_one, one_ref)):
        wide = jnp.concatenate(
            [
                weight_ref[...].astype(jnp.float32),
                jnp.zeros((plan.cols, plan.depth * LANES - plan.rows), jnp.float32),
            ],
            axis=1,
        )
        share_ref[...] = pltpu.roll(wide, offset, 1).astype(jnp.bfloat16)
    for copy in copies:
        copy.wait()
    for side, strip_ref in enumerate((first_x, last_x, first_y, last_y)):
        for part in range(n_by if side < 2 else n_bx):
            at = ((0, part), (n_bx - 1, part), (part, 0), (part, n_by - 1))[side]
            rows = slice(part * B, (part + 1) * B)
            for index in range(3):
                value = raw_ref[side, index, rows].astype(jnp.float32)
                if index == 0:
                    value = jnp.maximum(value, 0.0)
                value = jnp.where(occ_ref[at[0], 0, at[1]] > 0, value, 0.0)
                strip_ref[index, rows] = value.astype(jnp.bfloat16)


def first_steps(plan, occ, weight_two, weight_one, fields, n_bx, n_by):
    size_x, size_y, edge, chans = fields[0].shape
    smem = pl.BlockSpec(memory_space=pltpu.SMEM)
    anywhere = pl.BlockSpec(memory_space=pl.ANY)
    vmem = pl.BlockSpec(memory_space=pltpu.VMEM)
    share = jax.ShapeDtypeStruct((plan.cols, plan.depth * LANES), jnp.bfloat16)
    along_y = jax.ShapeDtypeStruct((3, size_y, edge, chans), jnp.bfloat16)
    along_x = jax.ShapeDtypeStruct((3, size_x, edge, chans), jnp.bfloat16)
    return pl.pallas_call(
        functools.partial(first_kernel, plan, n_bx, n_by),
        out_shape=[share, share, along_y, along_y, along_x, along_x],
        in_specs=[smem, vmem, vmem] + [anywhere] * 3,
        out_specs=[vmem] * 6,
        scratch_shapes=[
            pltpu.VMEM((4, 3, max(size_x, size_y), edge, chans), jnp.bfloat16),
            pltpu.SemaphoreType.DMA((4, 3)),
        ],
        cost_estimate=SMALL,
    )(occ, weight_two.T, weight_one.T, *fields)


class Gathered:
    def __init__(self, array, distances):
        self.array = array
        self.distances = distances

    def from_others(self, plan, flips):
        return [
            Gathered(
                swap(self.array, plan, flip_gx, flip_gy),
                [(i ^ flip_gx, j ^ flip_gy) for i, j in self.distances],
            )
            for flip_gx, flip_gy in flips
        ]

    def joined(self, others):
        parts = [self] + others
        return Gathered(
            jnp.concatenate([part.array for part in parts], axis=0),
            [distance for part in parts for distance in part.distances],
        )

    def part(self, start, stop):
        return Gathered(self.array[start:stop], self.distances[start:stop])

    def after(self, *others):
        return Gathered(after(self.array, *others), self.distances)


def plane_flips(plan):
    return [
        (slot // plan.inner * plan.pair, slot % plan.inner) for slot in range(1, plan.n_plane)
    ]


def z_steps(plan):
    step = plan.n_z // 2
    while step > 0:
        yield [(0, step * plan.inner)]
        step //= 2


def both_cores(plan, gathered):
    return [gathered] + gathered.from_others(plan, [(1, 0)])


class Halving:
    def __init__(self, plan, sums):
        self.plan = plan
        bits = [1 << i for i in range(plan.n_plane.bit_length() - 1)]
        self.orders = [bits, bits[1:] + bits[:1]]
        half = plan.n_z // 2
        self.slots = [list(range(plan.n_plane))] * 2
        self.parts = [sums[:, :half], sums[:, half:]]
        self.step = 0

    def sends(self):
        out = []
        for half in range(2):
            bit = self.orders[half][self.step]
            away = [i for i, slot in enumerate(self.slots[half]) if slot & bit]
            out.append(take(self.parts[half], away).astype(jnp.bfloat16))
        return out

    def swaps(self, sends):
        out = []
        for half in range(2):
            slot = self.orders[half][self.step]
            plan = self.plan
            out.append(
                swap(sends[half], plan, slot // plan.inner * plan.pair, slot % plan.inner)
            )
        return out

    def add(self, got):
        for half in range(2):
            bit = self.orders[half][self.step]
            stay = [i for i, slot in enumerate(self.slots[half]) if not slot & bit]
            kept = take(self.parts[half], stay).astype(jnp.float32)
            self.parts[half] = kept + got[half].astype(jnp.float32)
            self.slots = list(self.slots)
            self.slots[half] = [self.slots[half][i] for i in stay]
        self.step += 1

    def last(self):
        return self.step + 1 == len(self.orders[0])

    def done(self):
        return self.step == len(self.orders[0])

    def line(self):
        return jnp.concatenate([part[0] for part in self.parts], axis=0)


def take(array, indices):
    return jnp.concatenate([array[i : i + 1] for i in indices], axis=0)


def halve_z_step(plan, line, step):
    got = swap_z(line[1::2].astype(jnp.bfloat16), plan, step)
    return line[0::2].astype(jnp.float32) + got.astype(jnp.float32)


def spread_z(plan, line, *before):
    got = [
        swap_z(line[slot].astype(jnp.bfloat16), plan, slot) for slot in range(1, plan.n_z)
    ]
    own = line[0]
    for part in after(got, *before):
        own = own + part.astype(jnp.float32)
    return own


def finished(plan, own):
    scale = float(plan.n_gx * plan.n_gy * B**3) ** (-0.5)
    flat = (own * scale).transpose(1, 0, 2).reshape(plan.cols, plan.depth * LANES)
    offset = lax.axis_index("gx") * plan.rows % LANES
    return lax.dynamic_slice(flat, (0, offset), (plan.cols, plan.rows)).T


def ring(axis):
    size = lax.axis_size(axis)
    up = [(i, i + 1) for i in range(size - 1)]
    return up, [(j, i) for i, j in up]


def rims_x(first_x, last_x):
    up, down = ring("gx")
    return lax.ppermute(last_x, "gx", up), lax.ppermute(first_x, "gx", down)


def strips_y(low_x, high_x, first_y, last_y):
    return (
        jnp.concatenate([low_x[:, :1], first_y, high_x[:, :1]], axis=1),
        jnp.concatenate([low_x[:, -1:], last_y, high_x[:, -1:]], axis=1),
    )


def rims_y(first_y, last_y):
    up, down = ring("gy")
    return lax.ppermute(last_y, "gy", up), lax.ppermute(first_y, "gy", down)


def body(inputs, preact, out_grad, weight_one, weight_two, occupancy):
    n_bx, n_by = occupancy.shape[:2]
    plan = Plan(
        lax.axis_size("gx"), lax.axis_size("gy"), weight_one.shape[0], inputs.shape[-1]
    )
    occ = occupancy.transpose(0, 2, 1)

    own_two, own_one, first_x, last_x, first_y, last_y = first_steps(
        plan, occ, weight_two, weight_one, (preact, inputs, out_grad), n_bx, n_by
    )
    low_x, high_x = rims_x(first_x, last_x)
    steps = list(z_steps(plan))
    two = Gathered(own_two[None], [(0, 0)])
    for flips in steps[:-1]:
        two = two.joined(two.from_others(plan, flips))
    sent_y = after(strips_y(low_x, high_x, first_y, last_y), two.array)
    for flips in steps[-1:]:
        two = two.joined(two.from_others(plan, flips))
    one = Gathered(own_one[None], [(0, 0)]).after(sent_y)
    one = one.joined(one.from_others(plan, plane_flips(plan)))
    edges = after((low_x, high_x) + rims_y(*sent_y), one.array, two.array)
    two = two.after(edges)
    patches = patches_of(occ, (preact, inputs, out_grad), edges, n_bx, n_by)
    other = swap(patches, plan, 1, 0)
    sums_two = weight_sums(plan, 0, patches, other)
    for flips in steps[:-1]:
        one = one.joined([part.after(sums_two) for part in one.from_others(plan, flips)])
    others = two.from_others(plan, plane_flips(plan))
    two = two.joined([part.after(sums_two) for part in others]).after(one.array)
    halving_two = Halving(plan, sums_two)
    sends = after(halving_two.sends(), two.array)
    got_two = halving_two.swaps(sends)
    pieces = both_cores(plan, two)
    grad_one, center = data_grad(
        plan, occ, inputs.shape, [patches], after([part.array for part in pieces], sends),
        [part.distances for part in pieces], n_bx, n_by, preact,
    )
    other_center = swap(center, plan, 1, 0)
    halving_two.add(after(got_two, grad_one))
    while not halving_two.done():
        sends = halving_two.sends()
        got_two = halving_two.swaps(sends)
        if halving_two.last():
            sums_one = weight_sums(plan, 1, patches, other, (after(center, sends), other_center))
            got_two = after(got_two, sums_one)
        halving_two.add(got_two)
    for flips in steps[-1:]:
        others = one.after(two.array).from_others(plan, flips)
        one = one.joined([part.after(sums_one) for part in others])
    line_two = halving_two.line()

    halving_one = Halving(plan, after(sums_one, got_two))
    sends = halving_one.sends()
    got_one = halving_one.swaps(sends)
    line_two = halve_z_step(plan, after(line_two, sends), 1)
    strips = (grad_one[None, 0], grad_one[None, -1], grad_one[None, :, 0], grad_one[None, :, -1])
    strips = after(strips, sends)
    low_x, high_x = rims_x(*strips[:2])
    sent_y = strips_y(low_x, high_x, *strips[2:])
    halving_one.add(after(got_one, sent_y))
    while not halving_one.done():
        sends = halving_one.sends()
        got_one = halving_one.swaps(sends)
        if halving_one.last():
            line_two = after(line_two, sends)
            while line_two.shape[0] > 1:
                line_two = halve_z_step(plan, line_two, plan.n_z // line_two.shape[0])
            edges_one = (low_x, high_x) + rims_y(*after(sent_y, sends))
            got_one = after(got_one)
        halving_one.add(got_one)
    line_one = halving_one.line()
    pieces = both_cores(plan, one)
    (input_grad,) = data_grad(
        plan, occ, inputs.shape, (after(grad_one, line_one),) + edges_one,
        [part.array for part in pieces], [part.distances for part in pieces], n_bx, n_by,
    )
    own_one = spread_z(plan, line_one, input_grad)
    return (input_grad, finished(plan, own_one), finished(plan, line_two[0]))


def solution(mesh):
    return jax.shard_map(
        body,
        mesh=mesh,
        in_specs=(
            P("gx", "gy", None, None),
            P("gx", "gy", None, None),
            P("gx", "gy", None, None),
            P("gx", "gy"),
            P("gx", "gy"),
            P("gx", "gy", None),
        ),
        out_specs=(P("gx", "gy", None, None), P("gx", "gy"), P("gx", "gy")),
        check_vma=False,
    )
```
